128 devices in a mesh: req: 8 (over x, core), score: 16 (over y, z).
Axes of the slice: x: 4, y: 4, z: 4, core: 2. Of those that a mesh axis runs over, the one named last changes fastest.
Arguments:
- owner_ids: int32 [8, 16, 4, 256, 1], P('req', 'score'), may hold values from 0 to 127; in each aligned block of 256 rows (0 to 255, 256 to 511, ..., all dimensions but the last counted through in order) at most 3 rows name the same one
- local_rows: int32 [4, 32, 1024], P(None, 'req', 'score'), may hold values from 0 to 16383
- item_table: bfloat16 [2097152, 256], P(('req', 'score')), may hold values from -6 to 6
- user_feats: bfloat16 [4, 32, 1024], P(None, 'req'), may hold values from -6 to 6
- tower_in: bfloat16 [1024, 2048], P(None, 'score'), may hold values from -0.1875 to 0.1875
- tower_out: bfloat16 [2048, 256], P('score'), may hold values from -0.1875 to 0.1875
- cross_weights: bfloat16 [3, 512, 512], replicated, may hold values from -0.25 to 0.25
- mlp_in: bfloat16 [512, 2048], replicated, may hold values from -0.25 to 0.25
- mlp_mid: bfloat16 [2048, 2048], replicated, may hold values from -0.1875 to 0.1875
- mlp_out: bfloat16 [2048], replicated, may hold values from -0.1875 to 0.1875
Outputs:
- logits: float32 [4, 32, 1024], P(None, 'req', 'score')
The draws below stay inside these ranges and needn't reach their ends.
Inputs may be any that keep to these rules, and one draw needn't show every extreme that they name: Within one window of one device, the 256 candidates of owner_ids[i, j, w] (aligned blocks), no owner is named more than 3 times.
All inputs are finite; a program needn't handle non-finite values.
Results may differ from the reference program's by a relative error of at most 0.013.
Values may be sent and summed in bfloat16 or wider, within the bound.
A program may use at most 128 MiB of HBM per device.

```python
import math
import jax
import jax.numpy as jnp
import numpy as np
from jax import lax

D_ITEM = 256
D_USER = 256
D_IN = 512
USER_FEAT = 1024
TOWER_HID = 2048
HID = 2048
CROSS = 3
WINDOWS = 4
REQ_DEV = 4
CAND_DEV = 64
MOST = 3
ROWS_DEV = 16384
REQUESTS = 32
CANDIDATES = 1024
TABLE_ROWS = 2097152
N_REQ = 8
N_SCORE = 16
DEVICES = 128


def plant(result, own_key, smallest, high):
    shape = result.shape
    place = [jax.random.randint(jax.random.fold_in(own_key, axis), (), 0, shape[axis]) for axis in range(len(shape))]
    result = result.at[tuple(place)].set(smallest)
    longest = shape.index(max(shape))
    place[longest] = (place[longest] + 1) % shape[longest]
    return result.at[tuple(place)].set(high)


def level_of(own_key, extent, pieces, low, high):
    level, own = 1.0, jax.random.fold_in(own_key, 6)
    for axis_at, parts in pieces:
        heights = jnp.exp(jax.random.uniform(jax.random.fold_in(own, axis_at), (parts,), jnp.float32, low / len(pieces), high / len(pieces)))
        level = level * jnp.repeat(heights, extent[axis_at] // parts).reshape([-1 if axis == axis_at else 1 for axis in range(len(extent))])
    return level


def rank_table(amount, skew):
    weights = [(1 << 20) // math.isqrt(grade ** skew) + 1 for grade in range(1, amount + 1)]
    deviation = 1 + sum(weights) // (1 << 30)
    return np.cumsum(np.array([max(1, weight // deviation) for weight in weights]))


def ranked(rng, dims, amount, slope):
    listing = rank_table(amount, slope)
    ticket = jax.random.randint(jax.random.fold_in(rng, 1), dims, 0, int(listing[amount - 1]))
    grade = jnp.searchsorted(jnp.asarray(listing, jnp.int32), ticket, side="right")
    return jax.random.permutation(jax.random.fold_in(rng, 2), amount)[grade].astype(jnp.int32)


def shared_out(own_key, own, number, rows, number_of, top, reach, skew):
    order = jax.random.permutation(own_key, number_of)
    heavy_load, ordinary = portions_of(number_of, rows * top, reach, skew, True), portions_of(number_of, rows * top, reach, skew, False)
    places = jnp.arange(number_of)

    def named(sizes, offset_by):
        used = int((sizes > 0).sum())
        fixed = max(1, used // 4)
        moved = fixed + (places - fixed + offset_by * (used - fixed)) % max(1, number_of - fixed)
        return jnp.zeros((number_of,), jnp.int32).at[order[jnp.where(places < fixed, places, moved)]].set(jnp.asarray(sizes, jnp.int32))

    sizes = jnp.where(number % 4 == 0, named(heavy_load, number // 4), named(ordinary, number - number // 4 - 1))
    mixed = jax.random.permutation(jax.random.fold_in(own, 3), number_of)
    donor, receiver = mixed[0:number_of // 2 * 2:2], mixed[1:number_of // 2 * 2:2]
    slack = jnp.minimum(sizes[donor] - 1, reach - sizes[receiver]) // 2
    slack = jnp.where((donor == order[0]) | (receiver == order[0]) | (sizes[receiver] == 0), 0, jnp.maximum(slack, 0))
    moved = jax.random.randint(jax.random.fold_in(own, 4), (number_of // 2,), 0, 1 << 20) % (slack + 1)
    sizes = sizes.at[donor].add(-moved).at[receiver].add(moved)
    labels = jnp.searchsorted(jnp.cumsum(sizes), jnp.arange(rows * top), side="right").astype(jnp.int32)
    grid = labels.reshape(top, rows).T
    grid = grid[jax.random.permutation(jax.random.fold_in(own, 1), rows)]
    offset_by = jax.random.randint(jax.random.fold_in(own, 2), (rows, 1), 0, top)
    return jnp.take_along_axis(grid, (jnp.arange(top)[None, :] + offset_by) % top, axis=1)


def portions_of(number_of, total, limit, slope, full):
    weights = [(1 << 20) // math.isqrt(grade ** slope) + 1 for grade in range(1, number_of + 1)]
    largest = limit if full else min(limit, max(-(-total // number_of), total * weights[0] // sum(weights)))
    least = 1 if total - largest >= number_of - 1 else 0
    counts, spare = [largest] + [least] * (number_of - 1), total - largest - least * (number_of - 1)
    while spare > 0:
        free = [i for i in range(1, number_of) if counts[i] < largest] or [i for i in range(1, number_of) if counts[i] < limit]
        whole, left = sum([weights[i] for i in free]), spare
        for i in free:
            more = min(limit - counts[i], max(1, left * weights[i] // whole), spare)
            counts[i] = counts[i] + more
            spare = spare - more
    return np.array(counts)


def normal_values(own_key, dims, spread, limit, shards=(), held_as=jnp.bfloat16):
    values = jax.random.normal(own_key, dims, jnp.float32) * spread
    if len(shards) > 0:
        values = level_of(own_key, dims, shards, -0.22, 0.18) * values
    return jnp.clip(values, min=-limit, max=limit).astype(held_as)


def setup_inputs(seed: int = 0) -> dict:
    seeds = jax.random.split(jax.random.key(seed), 11)
    owner_ids_keys = jax.random.split(jax.random.fold_in(seeds[0], 1), N_REQ * N_SCORE * WINDOWS * (REQ_DEV * CAND_DEV) // (REQ_DEV * CAND_DEV))
    owner_ids_turns = jax.random.permutation(jax.random.fold_in(seeds[0], 3), N_REQ * N_SCORE * WINDOWS * (REQ_DEV * CAND_DEV) // (REQ_DEV * CAND_DEV))
    owner_ids = jax.vmap(lambda own, number: shared_out(jax.random.fold_in(seeds[0], 2), own, number, REQ_DEV * CAND_DEV, DEVICES, 1, MOST, 2))(owner_ids_keys, owner_ids_turns).reshape((N_REQ, N_SCORE, WINDOWS, REQ_DEV * CAND_DEV, 1))
    local_rows = plant(ranked(seeds[1], (WINDOWS, REQUESTS, CANDIDATES), ROWS_DEV, 2), jax.random.fold_in(seeds[1], 3), 0, ROWS_DEV - 1).astype(jnp.int32)
    item_table = normal_values(seeds[2], (TABLE_ROWS, D_ITEM), 1.0, 6.0, ((0, 128),))
    user_feats = normal_values(seeds[3], (WINDOWS, REQUESTS, USER_FEAT), 1.0, 6.0, ((1, 8),))
    tower_in = normal_values(seeds[4], (USER_FEAT, TOWER_HID), USER_FEAT ** -0.5, 0.1875, ((1, 16),))
    tower_out = normal_values(seeds[5], (TOWER_HID, D_USER), (TOWER_HID // 2) ** -0.5, 0.1875, ((0, 16),))
    cross_weights = normal_values(seeds[6], (CROSS, D_IN, D_IN), D_IN ** -0.5, 0.25)
    mlp_in = normal_values(seeds[7], (D_IN, HID), D_IN ** -0.5, 0.25)
    mlp_mid = normal_values(seeds[8], (HID, HID), (HID // 2) ** -0.5, 0.1875)
    mlp_out = normal_values(seeds[9], (HID,), (HID // 2) ** -0.5, 0.1875)
    return {"owner_ids": owner_ids, "local_rows": local_rows, "item_table": item_table, "user_feats": user_feats, "tower_in": tower_in, "tower_out": tower_out, "cross_weights": cross_weights, "mlp_in": mlp_in, "mlp_mid": mlp_mid, "mlp_out": mlp_out}


def score_window(embedded, user, cross_weights, mlp_in, mlp_mid, mlp_out):
    requests, candidates, width = embedded.shape
    user_rows = jnp.broadcast_to(user[:, None, :], (requests, candidates, user.shape[-1]))
    base = jnp.concatenate([embedded, user_rows], axis=-1).reshape(requests * candidates, -1)
    base_float = base.astype(jnp.float32)
    state = base_float
    for layer in range(CROSS):
        mixed = jnp.dot(state.astype(jnp.bfloat16), cross_weights[layer], preferred_element_type=jnp.float32)
        state = base_float * mixed + state
    first = jax.nn.relu(jnp.dot(state.astype(jnp.bfloat16), mlp_in, preferred_element_type=jnp.float32)).astype(jnp.bfloat16)
    second = jax.nn.relu(jnp.dot(first, mlp_mid, preferred_element_type=jnp.float32)).astype(jnp.bfloat16)
    logits = jnp.dot(second, mlp_out, preferred_element_type=jnp.float32)
    return logits.reshape(requests, candidates)


def reference(owner_ids, local_rows, item_table, user_feats, tower_in, tower_out, cross_weights, mlp_in, mlp_mid, mlp_out):
    owner = owner_ids[..., 0].reshape(N_REQ, N_SCORE, WINDOWS, REQ_DEV, CAND_DEV)
    owner = jnp.transpose(owner, (2, 0, 3, 1, 4)).reshape(WINDOWS, REQUESTS, CANDIDATES)
    item = (owner * ROWS_DEV + local_rows).astype(jnp.int32)
    windows, requests, features = user_feats.shape
    tower_hidden = jax.nn.relu(jnp.dot(user_feats.reshape(windows * requests, features), tower_in, preferred_element_type=jnp.float32)).astype(jnp.bfloat16)
    user = jnp.dot(tower_hidden, tower_out, preferred_element_type=jnp.float32).astype(jnp.bfloat16).reshape(windows, requests, -1)

    def one_window(inputs):
        item_window, user_window = inputs
        embedded = jnp.take(item_table, item_window, axis=0)
        return score_window(embedded, user_window, cross_weights, mlp_in, mlp_mid, mlp_out)

    return lax.map(one_window, (item, user))
```

```python
import functools

import jax
import jax.numpy as jnp
from jax import lax
from jax.experimental import pallas as pl
from jax.experimental.pallas import tpu as pltpu
from jax.sharding import PartitionSpec as P

CROSS = 3
WINDOWS = 4
BLOCK = 256
REQ_ROWS = 4
CAND = 64
MOST = 3
OWNERS = 128
ROWS = 16384
ITEM = 256
USER = 256
HID = 2048
HALF = 2 * BLOCK
SLOTS = 8
USED = 2 * MOST
CHUNKS = 8
MESH = pl.DeviceIdType.MESH
F32 = jnp.float32
BF16 = jnp.bfloat16


def peer(step):
    req, score = lax.axis_index("req"), lax.axis_index("score")
    turn = (step * 37) % 128
    z = (score % 4 + turn % 4) % 4
    y = (score // 4 + (turn // 4) % 4) % 4
    core = (req % 2 + (turn // 16) % 2) % 2
    x = (req // 2 + turn // 32) % 4
    return x * 2 + core, y * 4 + z


def kernel(
    owner_ref, rows_ref, feats_ref, out_w_ref,
    table_hbm, tin_hbm, tout_hbm, cross_hbm, win_hbm, wmid_hbm,
    logits_ref,
    table, table32, tin, tout, cross, win, wmid,
    ask, asked, asked_s, stage, give, got, part, parts, pick, first,
    load_sem, weight_sem, own_sem, ask_send, ask_recv, user_send, user_recv, row_send, row_recv,
):
    req, score = lax.axis_index("req"), lax.axis_index("score")
    me = req * 16 + score
    chunk = ROWS // CHUNKS

    small = [
        pltpu.make_async_copy(tin_hbm, tin, weight_sem.at[0]),
        pltpu.make_async_copy(tout_hbm, tout, weight_sem.at[1]),
    ]
    large = [
        pltpu.make_async_copy(cross_hbm, cross, weight_sem.at[2]),
        pltpu.make_async_copy(win_hbm, win, weight_sem.at[3]),
        pltpu.make_async_copy(wmid_hbm, wmid, weight_sem.at[4]),
    ]
    loads = [
        pltpu.make_async_copy(
            table_hbm.at[pl.ds(k * chunk, chunk)], table.at[pl.ds(k * chunk, chunk)], load_sem.at[k]
        )
        for k in range(CHUNKS)
    ]
    for copy in small + loads + large:
        copy.start()

    barrier = pltpu.get_barrier_semaphore()

    def greet(step, carry):
        to_req, to_score = peer(step)
        pl.semaphore_signal(barrier, inc=1, device_id=(to_req, to_score), device_id_type=MESH)
        return carry

    lax.fori_loop(1, OWNERS, greet, 0)

    tri_row = lax.broadcasted_iota(jnp.int32, (BLOCK, BLOCK), 0)
    tri_col = lax.broadcasted_iota(jnp.int32, (BLOCK, BLOCK), 1)
    earlier = jnp.where(tri_row < tri_col, 1.0, 0.0).astype(BF16)
    owner_iota = lax.broadcasted_iota(jnp.int32, (OWNERS, BLOCK), 0)
    high_sum = jnp.zeros((OWNERS, 128), F32)
    low_sum = jnp.zeros((OWNERS, 128), F32)
    places = []
    for w in range(WINDOWS):
        owner = owner_ref[pl.ds(w, 1), :]
        rows = rows_ref[pl.ds(w, 1), :]
        hot = jnp.where(owner_iota == owner, 1.0, 0.0)
        hot16 = hot.astype(BF16)
        before = jnp.dot(hot16, earlier, preferred_element_type=F32)
        slot = jnp.sum(before * hot, axis=0, keepdims=True).astype(jnp.int32)
        at_slot = owner_iota == slot + w * MOST
        high = jnp.where(at_slot, (rows // 128).astype(F32), 0.0).astype(BF16)
        low = jnp.where(at_slot, (rows % 128).astype(F32), 0.0).astype(BF16)
        contract = (((1,), (1,)), ((), ()))
        high_sum += lax.dot_general(hot16, high, contract, preferred_element_type=F32)
        low_sum += lax.dot_general(hot16, low, contract, preferred_element_type=F32)
        places.append(owner * SLOTS + slot + (w % 2) * MOST)
    asks = (high_sum * 128.0 + low_sum).astype(jnp.int32) * 2
    ask[...] = asks.reshape(OWNERS, 1, 128)

    pl.semaphore_wait(barrier, OWNERS - 1)

    def send_ask(step, carry):
        to_req, to_score = peer(step)
        pltpu.make_async_remote_copy(
            src_ref=ask.at[to_req * 16 + to_score],
            dst_ref=asked.at[me],
            send_sem=ask_send,
            recv_sem=ask_recv,
            device_id=(to_req, to_score),
            device_id_type=MESH,
        ).start()
        return carry

    lax.fori_loop(1, OWNERS, send_ask, 0)
    asked[pl.ds(me, 1)] = ask[pl.ds(me, 1)]

    for copy in small:
        copy.wait()
    feats = jnp.concatenate([feats_ref[w].astype(F32) for w in range(WINDOWS)], axis=0).astype(BF16)
    hidden = jnp.maximum(jnp.dot(feats, tin[...], preferred_element_type=F32), 0.0).astype(BF16)
    part[...] = jnp.dot(hidden, tout[...], preferred_element_type=F32)

    def send_part(step, carry):
        pltpu.make_async_remote_copy(
            src_ref=part,
            dst_ref=parts.at[score],
            send_sem=user_send,
            recv_sem=user_recv,
            device_id=(req, (score + step) % 16),
            device_id_type=MESH,
        ).start()
        return carry

    lax.fori_loop(1, 16, send_part, 0)
    parts[pl.ds(score, 1)] = part[...][None]

    for k in range(CHUNKS):
        loads[k].wait()

        def widen(step, carry):
            base = pl.multiple_of(k * chunk + step * 64, 64)
            block = table[pl.ds(base, 64), :].astype(F32)
            table32[pl.ds(2 * base, 64, stride=2), :] = block[:, :128]
            table32[pl.ds(2 * base + 1, 64, stride=2), :] = block[:, 128:]
            return carry

        lax.fori_loop(0, chunk // 64, widen, 0)

    place = jnp.concatenate(places + [jnp.zeros((4, BLOCK), jnp.int32)], axis=0)
    place_t = place.T
    lane = lax.broadcasted_iota(jnp.int32, (BLOCK, OWNERS * SLOTS), 1)
    for w in range(WINDOWS):
        pick[w * BLOCK:(w + 1) * BLOCK, :] = jnp.where(
            lane == place_t[:, w:w + 1], 1.0, 0.0
        ).astype(BF16)

    everything = asked.at[pl.ds(0, OWNERS - 1)]
    pltpu.make_async_copy(everything, everything, ask_recv).wait()
    to_smem = pltpu.make_async_copy(asked, asked_s, own_sem.at[0])
    to_smem.start()

    def clear(step, carry):
        stage[pl.ds(pl.multiple_of(step * 64, 64), 64), :] = jnp.zeros((64, 128), F32)
        return carry

    lax.fori_loop(0, 2 * OWNERS * 2 * SLOTS // 64, clear, 0)
    to_smem.wait()

    def look_up(half, to):
        base = pl.multiple_of((half * OWNERS + to) * 2 * SLOTS, 2 * SLOTS)
        for s in range(USED):
            at = jnp.clip(asked_s[to, 0, half * USED + s], 0, 2 * ROWS - 2)
            stage[pl.ds(base + 2 * s, 2), :] = table32[pl.ds(at, 2), :]
        give[half, to, 0:SLOTS, :] = stage[pl.ds(base, SLOTS, stride=2), :].astype(BF16)
        give[half, to, SLOTS:2 * SLOTS, :] = stage[pl.ds(base + 1, SLOTS, stride=2), :].astype(BF16)

    for half in range(2):

        def send_rows(step, carry):
            to_req, to_score = peer(step)
            to = to_req * 16 + to_score
            look_up(half, to)
            pltpu.make_async_remote_copy(
                src_ref=give.at[half, to],
                dst_ref=got.at[half, me],
                send_sem=row_send.at[half],
                recv_sem=row_recv.at[half],
                device_id=(to_req, to_score),
                device_id_type=MESH,
            ).start()
            return carry

        lax.fori_loop(1, OWNERS, send_rows, 0)
        look_up(half, me)
        got[half, pl.ds(me, 1)] = give[half, pl.ds(me, 1)]

    fifteen = parts.at[pl.ds(0, 15)]
    pltpu.make_async_copy(fifteen, fifteen, user_recv).wait()
    user = jnp.sum(parts[...], axis=0).astype(BF16)
    for copy in large:
        copy.wait()
    user_mixed = jnp.dot(user, cross[0, ITEM:, :], preferred_element_type=F32)
    user32 = user.astype(F32)

    def spread(rows, half):
        width = rows.shape[1]
        return jnp.concatenate(
            [jnp.broadcast_to(rows[q:q + 1], (CAND, width)) for q in range(8 * half, 8 * half + 8)],
            axis=0,
        )

    for half in range(2):
        arrived = got.at[half, pl.ds(0, OWNERS - 1)]
        pltpu.make_async_copy(arrived, arrived, row_recv.at[half]).wait()
        left = got[half, :, 0:SLOTS, :].reshape(OWNERS * SLOTS, 128)
        right = got[half, :, SLOTS:2 * SLOTS, :].reshape(OWNERS * SLOTS, 128)
        found = jnp.concatenate([left, right], axis=1)
        embedded = jnp.dot(
            pick[half * HALF:(half + 1) * HALF, :], found, preferred_element_type=F32
        )
        base = jnp.concatenate([embedded, spread(user32, half)], axis=1)
        mixed = jnp.dot(
            embedded.astype(BF16), cross[0, :ITEM, :], preferred_element_type=F32
        ) + spread(user_mixed, half)
        state = base * mixed + base
        for layer in range(1, CROSS):
            mixed = jnp.dot(state.astype(BF16), cross[layer], preferred_element_type=F32)
            state = base * mixed + state
        state16 = state.astype(BF16)

        def deep_in(n, carry):
            columns = pl.ds(pl.multiple_of(n * 256, 256), 256)
            value = jnp.dot(state16, win[:, columns], preferred_element_type=F32)
            first[:, columns] = jnp.maximum(value, 0.0).astype(BF16)
            return carry

        lax.fori_loop(0, HID // 256, deep_in, 0)

        def deep_mid(n, total):
            columns = pl.ds(pl.multiple_of(n * 256, 256), 256)
            value = jnp.dot(first[...], wmid[:, columns], preferred_element_type=F32)
            second = jnp.maximum(value, 0.0).astype(BF16).astype(F32) * out_w_ref[:, columns]
            return total + second[:, :128] + second[:, 128:]

        total = lax.fori_loop(0, HID // 256, deep_mid, jnp.zeros((HALF, 128), F32))
        scores = jnp.sum(total.T, axis=0, keepdims=True)
        for q in range(8):
            logits_ref[half * 2 + q // 4, pl.ds(q % 4, 1), :] = scores[:, q * CAND:(q + 1) * CAND]

    pltpu.make_async_copy(everything, everything, ask_send).wait()
    pltpu.make_async_copy(fifteen, fifteen, user_send).wait()
    for half in range(2):
        arrived = got.at[half, pl.ds(0, OWNERS - 1)]
        pltpu.make_async_copy(arrived, arrived, row_send.at[half]).wait()


def on_device(
    owner_ids, local_rows, item_table, user_feats, tower_in, tower_out,
    cross_weights, mlp_in, mlp_mid, mlp_out,
):
    vmem = pl.BlockSpec(memory_space=pltpu.VMEM)
    hbm = pl.BlockSpec(memory_space=pl.ANY)
    dma = pltpu.SemaphoreType.DMA
    return pl.pallas_call(
        kernel,
        out_shape=jax.ShapeDtypeStruct((WINDOWS, REQ_ROWS, CAND), F32),
        in_specs=[vmem] * 4 + [hbm] * 6,
        out_specs=vmem,
        scratch_shapes=[
            pltpu.VMEM((ROWS, ITEM), BF16),
            pltpu.VMEM((2 * ROWS + 8, 128), F32),
            pltpu.VMEM((1024, 128), BF16),
            pltpu.VMEM((128, USER), BF16),
            pltpu.VMEM((CROSS, 512, 512), BF16),
            pltpu.VMEM((512, HID), BF16),
            pltpu.VMEM((HID, HID), BF16),
            pltpu.VMEM((OWNERS, 1, 128), jnp.int32),
            pltpu.VMEM((OWNERS, 1, 128), jnp.int32),
            pltpu.SMEM((OWNERS, 1, 128), jnp.int32),
            pltpu.VMEM((2 * OWNERS * 2 * SLOTS + 8, 128), F32),
            pltpu.VMEM((2, OWNERS, 2 * SLOTS, 128), BF16),
            pltpu.VMEM((2, OWNERS, 2 * SLOTS, 128), BF16),
            pltpu.VMEM((16, USER), F32),
            pltpu.VMEM((16, 16, USER), F32),
            pltpu.VMEM((WINDOWS * BLOCK, OWNERS * SLOTS), BF16),
            pltpu.VMEM((HALF, HID), BF16),
            dma((CHUNKS,)),
            dma((5,)),
            dma((1,)),
            dma,
            dma,
            dma,
            dma,
            dma((2,)),
            dma((2,)),
        ],
        compiler_params=pltpu.CompilerParams(
            collective_id=0, has_side_effects=True, vmem_limit_bytes=60 * 1024 * 1024
        ),
        cost_estimate=pl.CostEstimate(
            flops=13_500_000_000, bytes_accessed=21_000_000, transcendentals=0
        ),
    )(
        owner_ids.reshape(WINDOWS, BLOCK),
        local_rows.reshape(WINDOWS, BLOCK),
        user_feats,
        mlp_out.astype(F32).reshape(1, HID),
        item_table,
        tower_in,
        tower_out,
        cross_weights,
        mlp_in,
        mlp_mid,
    )


def solution(mesh):
    in_specs = (
        P("req", "score", None, None, None),
        P(None, "req", "score"),
        P(("req", "score"), None),
        P(None, "req", None),
        P(None, "score"),
        P("score", None),
        P(),
        P(),
        P(),
        P(),
    )
    return jax.shard_map(
        on_device,
        mesh=mesh,
        in_specs=in_specs,
        out_specs=P(None, "req", "score"),
        check_vma=False,
    )
```

```python
import functools

import jax
import jax.numpy as jnp
from jax import lax
from jax.experimental import pallas as pl
from jax.experimental.pallas import tpu as pltpu
from jax.sharding import PartitionSpec as P

CROSS = 3
WINDOWS = 4
BLOCK = 256
REQ_ROWS = 4
CAND = 64
MOST = 3
OWNERS = 128
ROWS = 16384
ITEM = 256
USER = 256
HID = 2048
HALF = 2 * BLOCK
SLOTS = 8
USED = 2 * MOST
CHUNKS = 8
MESH = pl.DeviceIdType.MESH
F32 = jnp.float32
BF16 = jnp.bfloat16


def for_peers(visit, first=1):
    req, score = lax.axis_index("req"), lax.axis_index("score")
    core = req % 2
    x, y, z = req // 2, score // 4, score % 4
    xs = [((x + d) % 4) * 2 for d in range(4)]
    ys = [((y + d) % 4) * 4 for d in range(4)]
    zs = tuple((z + d) % 4 for d in range(4))

    def step(o, zs, start):
        here = jnp.where(o < 4, core, 1 - core)
        cores = (here, 1 - here)
        group = []
        for k in range(start, 16):
            dx, turn = k % 4, k // 4
            dy = (turn + dx) % 4
            group.append((k, xs[dx] + cores[(dx + turn) % 2], ys[dy] + zs[(turn + 2 * dx) % 4]))
        visit(o, group)
        return zs[1:] + zs[:1]

    zs = step(0, zs, first)
    lax.fori_loop(1, 8, lambda o, zs: step(o, zs, 0), zs)


def kernel(
    owner_ref, rows_ref, feats_ref, out_w_ref,
    table_hbm, tin_hbm, tout_hbm, cross_hbm, win_hbm, wmid_hbm,
    logits_ref,
    table, table32, tin, tout, cross, win, wmid,
    out_w, ask, asked, asked_s, stage, give, got, part, parts, pick, first,
    load_sem, weight_sem, own_sem, ask_send, ask_recv, user_send, user_recv, row_send, row_recv,
):
    req, score = lax.axis_index("req"), lax.axis_index("score")
    me = req * 16 + score
    chunk = ROWS // CHUNKS

    small = [
        pltpu.make_async_copy(tin_hbm, tin, weight_sem.at[0]),
        pltpu.make_async_copy(tout_hbm, tout, weight_sem.at[1]),
    ]
    large = [
        pltpu.make_async_copy(cross_hbm, cross, weight_sem.at[2]),
        pltpu.make_async_copy(win_hbm, win, weight_sem.at[3]),
        pltpu.make_async_copy(wmid_hbm, wmid, weight_sem.at[4]),
    ]
    loads = [
        pltpu.make_async_copy(
            table_hbm.at[pl.ds(k * chunk, chunk)], table.at[pl.ds(k * chunk, chunk)], load_sem.at[k]
        )
        for k in range(CHUNKS)
    ]
    for copy in small + loads + large:
        copy.start()

    barrier = pltpu.get_barrier_semaphore()

    def greet(o, group):
        for _, to_req, to_score in group:
            pl.semaphore_signal(barrier, inc=1, device_id=(to_req, to_score), device_id_type=MESH)

    for_peers(greet)

    tri_row = lax.broadcasted_iota(jnp.int32, (BLOCK, BLOCK), 0)
    tri_col = lax.broadcasted_iota(jnp.int32, (BLOCK, BLOCK), 1)
    earlier = jnp.where(tri_row < tri_col, 1.0, 0.0).astype(BF16)
    owner_iota = lax.broadcasted_iota(jnp.int32, (OWNERS, BLOCK), 0)
    high_sum = jnp.zeros((OWNERS, 128), F32)
    low_sum = jnp.zeros((OWNERS, 128), F32)
    places = []
    for w in range(WINDOWS):
        owner = owner_ref[w]
        rows = jnp.concatenate([rows_ref[w, r:r + 1, :] for r in range(REQ_ROWS)], axis=1)
        hot = jnp.where(owner_iota == owner, 1.0, 0.0)
        hot16 = hot.astype(BF16)
        before = jnp.dot(hot16, earlier, preferred_element_type=F32)
        slot = jnp.sum(before * hot, axis=0, keepdims=True).astype(jnp.int32)
        at_slot = owner_iota == slot + w * MOST
        high = jnp.where(at_slot, (rows // 128).astype(F32), 0.0).astype(BF16)
        low = jnp.where(at_slot, (rows % 128).astype(F32), 0.0).astype(BF16)
        contract = (((1,), (1,)), ((), ()))
        high_sum += lax.dot_general(hot16, high, contract, preferred_element_type=F32)
        low_sum += lax.dot_general(hot16, low, contract, preferred_element_type=F32)
        places.append(owner * SLOTS + slot + (w % 2) * MOST)
    asks = (high_sum * 128.0 + low_sum).astype(jnp.int32) * 2
    ask[...] = asks.reshape(OWNERS, 1, 128)

    pl.semaphore_wait(barrier, OWNERS - 1)

    def send_ask(o, group):
        for _, to_req, to_score in group:
            pltpu.make_async_remote_copy(
                src_ref=ask.at[to_req * 16 + to_score],
                dst_ref=asked.at[me],
                send_sem=ask_send,
                recv_sem=ask_recv,
                device_id=(to_req, to_score),
                device_id_type=MESH,
            ).start()

    for_peers(send_ask)
    asked[pl.ds(me, 1)] = ask[pl.ds(me, 1)]

    for copy in small:
        copy.wait()
    feats = jnp.concatenate([feats_ref[w].astype(F32) for w in range(WINDOWS)], axis=0).astype(BF16)
    hidden = jnp.maximum(jnp.dot(feats, tin[...], preferred_element_type=F32), 0.0).astype(BF16)
    part[...] = jnp.dot(hidden, tout[...], preferred_element_type=F32)

    def send_part(step, carry):
        pltpu.make_async_remote_copy(
            src_ref=part,
            dst_ref=parts.at[score],
            send_sem=user_send,
            recv_sem=user_recv,
            device_id=(req, (score + step) % 16),
            device_id_type=MESH,
        ).start()
        return carry

    lax.fori_loop(1, 16, send_part, 0)
    parts[pl.ds(score, 1)] = part[...][None]

    for k in range(CHUNKS):
        loads[k].wait()

        def widen(step, carry):
            base = pl.multiple_of(k * chunk + step * 64, 64)
            block = table[pl.ds(base, 64), :].astype(F32)
            table32[pl.ds(2 * base, 64, stride=2), :] = block[:, :128]
            table32[pl.ds(2 * base + 1, 64, stride=2), :] = block[:, 128:]
            return carry

        lax.fori_loop(0, chunk // 64, widen, 0)

    place = jnp.concatenate(places + [jnp.zeros((4, BLOCK), jnp.int32)], axis=0)
    place_t = place.T
    lane = lax.broadcasted_iota(jnp.int32, (BLOCK, OWNERS * SLOTS), 1)
    for w in range(WINDOWS):
        pick[w * BLOCK:(w + 1) * BLOCK, :] = jnp.where(
            lane == place_t[:, w:w + 1], 1.0, 0.0
        ).astype(BF16)

    everything = asked.at[pl.ds(0, OWNERS - 1)]
    pltpu.make_async_copy(everything, everything, ask_recv).wait()
    to_smem = pltpu.make_async_copy(asked, asked_s, own_sem.at[0])
    to_smem.start()

    stage[...] = jnp.zeros_like(stage)
    to_smem.wait()

    def look_up(half, to, slot, k):
        base = k * 2 * SLOTS
        for s in range(USED):
            at = jnp.clip(asked_s[to, 0, half * USED + s], 0, 2 * ROWS - 2)
            stage[base + 2 * s:base + 2 * s + 2, :] = table32[pl.ds(at, 2), :]
        give[half, slot, 0:SLOTS, :] = stage[pl.ds(base, SLOTS, stride=2), :].astype(BF16)
        give[half, slot, SLOTS:2 * SLOTS, :] = stage[pl.ds(base + 1, SLOTS, stride=2), :].astype(BF16)

    for half in range(2):

        def send_rows(o, group):
            for k, to_req, to_score in group:
                look_up(half, to_req * 16 + to_score, o * 16 + k, k)
            for k, to_req, to_score in group:
                pltpu.make_async_remote_copy(
                    src_ref=give.at[half, o * 16 + k],
                    dst_ref=got.at[half, me],
                    send_sem=row_send.at[half],
                    recv_sem=row_recv.at[half],
                    device_id=(to_req, to_score),
                    device_id_type=MESH,
                ).start()

        for_peers(send_rows)
        look_up(half, me, 0, 0)
        got[half, pl.ds(me, 1)] = give[half, 0:1]

    fifteen = parts.at[pl.ds(0, 15)]
    pltpu.make_async_copy(fifteen, fifteen, user_recv).wait()
    user = jnp.sum(parts[...], axis=0).astype(BF16)
    for copy in large:
        copy.wait()
    user_mixed = jnp.dot(user, cross[0, ITEM:, :], preferred_element_type=F32)
    user32 = user.astype(F32)
    out_w[...] = out_w_ref[...].astype(F32)

    def spread(rows, half):
        width = rows.shape[1]
        return jnp.concatenate(
            [jnp.broadcast_to(rows[q:q + 1], (CAND, width)) for q in range(8 * half, 8 * half + 8)],
            axis=0,
        )

    for half in range(2):
        arrived = got.at[half, pl.ds(0, OWNERS - 1)]
        pltpu.make_async_copy(arrived, arrived, row_recv.at[half]).wait()
        left = got[half, :, 0:SLOTS, :].reshape(OWNERS * SLOTS, 128)
        right = got[half, :, SLOTS:2 * SLOTS, :].reshape(OWNERS * SLOTS, 128)
        found = jnp.concatenate([left, right], axis=1)
        embedded = jnp.dot(
            pick[half * HALF:(half + 1) * HALF, :], found, preferred_element_type=F32
        )
        base = jnp.concatenate([embedded, spread(user32, half)], axis=1)
        mixed = jnp.dot(
            embedded.astype(BF16), cross[0, :ITEM, :], preferred_element_type=F32
        ) + spread(user_mixed, half)
        state = base * mixed + base
        for layer in range(1, CROSS):
            mixed = jnp.dot(state.astype(BF16), cross[layer], preferred_element_type=F32)
            state = base * mixed + state
        state16 = state.astype(BF16)

        def deep_in(n, carry):
            columns = pl.ds(pl.multiple_of(n * 256, 256), 256)
            value = jnp.dot(state16, win[:, columns], preferred_element_type=F32)
            first[:, columns] = jnp.maximum(value, 0.0).astype(BF16)
            return carry

        lax.fori_loop(0, HID // 256, deep_in, 0)

        def deep_mid(n, total):
            columns = pl.ds(pl.multiple_of(n * 256, 256), 256)
            value = jnp.dot(first[...], wmid[:, columns], preferred_element_type=F32)
            second = jnp.maximum(value, 0.0).astype(BF16).astype(F32)
            total += second[:, :128] * out_w[pl.ds(2 * n, 1), :]
            return total + second[:, 128:] * out_w[pl.ds(2 * n + 1, 1), :]

        total = lax.fori_loop(0, HID // 256, deep_mid, jnp.zeros((HALF, 128), F32))
        scores = jnp.sum(total.T, axis=0, keepdims=True)
        for q in range(8):
            logits_ref[half * 2 + q // 4, pl.ds(q % 4, 1), :] = scores[:, q * CAND:(q + 1) * CAND]

    pltpu.make_async_copy(everything, everything, ask_send).wait()
    pltpu.make_async_copy(fifteen, fifteen, user_send).wait()
    for half in range(2):
        arrived = got.at[half, pl.ds(0, OWNERS - 1)]
        pltpu.make_async_copy(arrived, arrived, row_send.at[half]).wait()


def on_device(
    owner_ids, local_rows, item_table, user_feats, tower_in, tower_out,
    cross_weights, mlp_in, mlp_mid, mlp_out,
):
    vmem = pl.BlockSpec(memory_space=pltpu.VMEM)
    hbm = pl.BlockSpec(memory_space=pl.ANY)
    dma = pltpu.SemaphoreType.DMA
    return pl.pallas_call(
        kernel,
        out_shape=jax.ShapeDtypeStruct((WINDOWS, REQ_ROWS, CAND), F32),
        in_specs=[vmem] * 4 + [hbm] * 6,
        out_specs=vmem,
        scratch_shapes=[
            pltpu.VMEM((ROWS, ITEM), BF16),
            pltpu.VMEM((2 * ROWS + 8, 128), F32),
            pltpu.VMEM((1024, 128), BF16),
            pltpu.VMEM((128, USER), BF16),
            pltpu.VMEM((CROSS, 512, 512), BF16),
            pltpu.VMEM((512, HID), BF16),
            pltpu.VMEM((HID, HID), BF16),
            pltpu.VMEM((HID // 128, 128), F32),
            pltpu.VMEM((OWNERS, 1, 128), jnp.int32),
            pltpu.VMEM((OWNERS, 1, 128), jnp.int32),
            pltpu.SMEM((OWNERS, 1, 128), jnp.int32),
            pltpu.VMEM((16 * 2 * SLOTS + 8, 128), F32),
            pltpu.VMEM((2, OWNERS, 2 * SLOTS, 128), BF16),
            pltpu.VMEM((2, OWNERS, 2 * SLOTS, 128), BF16),
            pltpu.VMEM((16, USER), F32),
            pltpu.VMEM((16, 16, USER), F32),
            pltpu.VMEM((WINDOWS * BLOCK, OWNERS * SLOTS), BF16),
            pltpu.VMEM((HALF, HID), BF16),
            dma((CHUNKS,)),
            dma((5,)),
            dma((1,)),
            dma,
            dma,
            dma,
            dma,
            dma((2,)),
            dma((2,)),
        ],
        compiler_params=pltpu.CompilerParams(
            collective_id=0, has_side_effects=True, vmem_limit_bytes=60 * 1024 * 1024
        ),
        cost_estimate=pl.CostEstimate(
            flops=13_500_000_000, bytes_accessed=21_000_000, transcendentals=0
        ),
    )(
        owner_ids.reshape(WINDOWS, 1, BLOCK),
        local_rows,
        user_feats,
        mlp_out.reshape(HID // 128, 128),
        item_table,
        tower_in,
        tower_out,
        cross_weights,
        mlp_in,
        mlp_mid,
    )


def solution(mesh):
    in_specs = (
        P("req", "score", None, None, None),
        P(None, "req", "score"),
        P(("req", "score"), None),
        P(None, "req", None),
        P(None, "score"),
        P("score", None),
        P(),
        P(),
        P(),
        P(),
    )
    return jax.shard_map(
        on_device,
        mesh=mesh,
        in_specs=in_specs,
        out_specs=P(None, "req", "score"),
        check_vma=False,
    )
```

```python
import functools

import jax
import jax.numpy as jnp
from jax import lax
from jax.experimental import pallas as pl
from jax.experimental.pallas import tpu as pltpu
from jax.sharding import PartitionSpec as P

CROSS = 3
WINDOWS = 4
BLOCK = 256
REQ_ROWS = 4
CAND = 64
MOST = 3
OWNERS = 128
ROWS = 16384
ITEM = 256
USER = 256
HID = 2048
HALF = 2 * BLOCK
SLOTS = 8
USED = 2 * MOST
CHUNKS = 8
MESH = pl.DeviceIdType.MESH
F32 = jnp.float32
BF16 = jnp.bfloat16


def for_peers(visit, first=1):
    req, score = lax.axis_index("req"), lax.axis_index("score")
    core = req % 2
    x, y, z = req // 2, score // 4, score % 4
    xs = [((x + d) % 4) * 2 for d in range(4)]
    ys = [((y + d) % 4) * 4 for d in range(4)]
    zs = tuple((z + d) % 4 for d in range(4))

    def step(o, zs, start):
        here = jnp.where(o < 4, core, 1 - core)
        cores = (here, 1 - here)
        group = []
        for k in range(start, 16):
            dx, turn = k % 4, k // 4
            dy = (turn + dx) % 4
            group.append((k, xs[dx] + cores[(dx + turn) % 2], ys[dy] + zs[(turn + 2 * dx) % 4]))
        visit(o, group)
        return zs[1:] + zs[:1]

    zs = step(0, zs, first)
    lax.fori_loop(1, 8, lambda o, zs: step(o, zs, 0), zs)


def kernel(
    owner_ref, rows_ref, feats_ref, out_w_ref,
    table_hbm, tin_hbm, tout_hbm, cross_hbm, win_hbm, wmid_hbm,
    logits_ref,
    table, table32, tin, tout, cross, win, wmid,
    out_w, ask, asked, asked_s, stage, give, got, part, parts, pick, first,
    load_sem, weight_sem, own_sem, ask_send, ask_recv, user_send, user_recv, row_send, row_recv,
):
    req, score = lax.axis_index("req"), lax.axis_index("score")
    me = req * 16 + score
    chunk = ROWS // CHUNKS

    small = [
        pltpu.make_async_copy(tin_hbm, tin, weight_sem.at[0]),
        pltpu.make_async_copy(tout_hbm, tout, weight_sem.at[1]),
    ]
    large = [
        pltpu.make_async_copy(cross_hbm, cross, weight_sem.at[2]),
        pltpu.make_async_copy(win_hbm, win, weight_sem.at[3]),
        pltpu.make_async_copy(wmid_hbm, wmid, weight_sem.at[4]),
    ]
    loads = [
        pltpu.make_async_copy(
            table_hbm.at[pl.ds(k * chunk, chunk)], table.at[pl.ds(k * chunk, chunk)], load_sem.at[k]
        )
        for k in range(CHUNKS)
    ]
    for copy in small + loads + large:
        copy.start()

    barrier = pltpu.get_barrier_semaphore()

    def greet(o, group):
        for _, to_req, to_score in group:
            pl.semaphore_signal(barrier, inc=1, device_id=(to_req, to_score), device_id_type=MESH)

    for_peers(greet)

    tri_row = lax.broadcasted_iota(jnp.int32, (BLOCK, BLOCK), 0)
    tri_col = lax.broadcasted_iota(jnp.int32, (BLOCK, BLOCK), 1)
    earlier = jnp.where(tri_row < tri_col, 1.0, 0.0).astype(BF16)
    owner_iota = lax.broadcasted_iota(jnp.int32, (OWNERS, BLOCK), 0)
    high_sum = jnp.zeros((OWNERS, 128), F32)
    low_sum = jnp.zeros((OWNERS, 128), F32)
    places = []
    for w in range(WINDOWS):
        owner = owner_ref[w]
        rows = jnp.concatenate([rows_ref[w, r:r + 1, :] for r in range(REQ_ROWS)], axis=1)
        hot = jnp.where(owner_iota == owner, 1.0, 0.0)
        hot16 = hot.astype(BF16)
        before = jnp.dot(hot16, earlier, preferred_element_type=F32)
        slot = jnp.sum(before * hot, axis=0, keepdims=True).astype(jnp.int32)
        at_slot = owner_iota == slot + w * MOST
        high = jnp.where(at_slot, (rows // 128).astype(F32), 0.0).astype(BF16)
        low = jnp.where(at_slot, (rows % 128).astype(F32), 0.0).astype(BF16)
        contract = (((1,), (1,)), ((), ()))
        high_sum += lax.dot_general(hot16, high, contract, preferred_element_type=F32)
        low_sum += lax.dot_general(hot16, low, contract, preferred_element_type=F32)
        places.append(owner * SLOTS + slot + (w % 2) * MOST)
    asks = (high_sum * 128.0 + low_sum).astype(jnp.int32) * 2
    ask[...] = asks.reshape(OWNERS, 1, 128)

    pl.semaphore_wait(barrier, OWNERS - 1)

    def send_ask(o, group):
        for _, to_req, to_score in group:
            pltpu.make_async_remote_copy(
                src_ref=ask.at[to_req * 16 + to_score],
                dst_ref=asked.at[me],
                send_sem=ask_send,
                recv_sem=ask_recv,
                device_id=(to_req, to_score),
                device_id_type=MESH,
            ).start()

    for_peers(send_ask)
    asked[pl.ds(me, 1)] = ask[pl.ds(me, 1)]

    for copy in small:
        copy.wait()
    feats = jnp.concatenate([feats_ref[w].astype(F32) for w in range(WINDOWS)], axis=0).astype(BF16)
    hidden = jnp.maximum(jnp.dot(feats, tin[...], preferred_element_type=F32), 0.0).astype(BF16)
    part[...] = jnp.dot(hidden, tout[...], preferred_element_type=F32)

    def send_part(step, carry):
        pltpu.make_async_remote_copy(
            src_ref=part,
            dst_ref=parts.at[score],
            send_sem=user_send,
            recv_sem=user_recv,
            device_id=(req, (score + step) % 16),
            device_id_type=MESH,
        ).start()
        return carry

    lax.fori_loop(1, 16, send_part, 0)
    parts[pl.ds(score, 1)] = part[...][None]

    for k in range(CHUNKS):
        loads[k].wait()

        def widen(step, carry):
            base = pl.multiple_of(k * chunk + step * 64, 64)
            block = table[pl.ds(base, 64), :].astype(F32)
            table32[pl.ds(2 * base, 64, stride=2), :] = block[:, :128]
            table32[pl.ds(2 * base + 1, 64, stride=2), :] = block[:, 128:]
            return carry

        lax.fori_loop(0, chunk // 64, widen, 0)

    place = jnp.concatenate(places + [jnp.zeros((4, BLOCK), jnp.int32)], axis=0)
    place_t = place.T
    lane = lax.broadcasted_iota(jnp.int32, (BLOCK, OWNERS * SLOTS), 1)
    for w in range(WINDOWS):
        pick[w * BLOCK:(w + 1) * BLOCK, :] = jnp.where(
            lane == place_t[:, w:w + 1], 1.0, 0.0
        ).astype(BF16)

    everything = asked.at[pl.ds(0, OWNERS - 1)]
    pltpu.make_async_copy(everything, everything, ask_recv).wait()
    to_smem = pltpu.make_async_copy(asked, asked_s, own_sem.at[0])
    to_smem.start()

    stage[...] = jnp.zeros_like(stage)
    to_smem.wait()

    def look_up(half, to, slot, k):
        base = k * 2 * SLOTS
        for s in range(USED):
            at = jnp.clip(asked_s[to, 0, half * USED + s], 0, 2 * ROWS - 2)
            stage[base + 2 * s:base + 2 * s + 2, :] = table32[pl.ds(at, 2), :]
        give[half, slot, 0:SLOTS, :] = stage[pl.ds(base, SLOTS, stride=2), :].astype(BF16)
        give[half, slot, SLOTS:2 * SLOTS, :] = stage[pl.ds(base + 1, SLOTS, stride=2), :].astype(BF16)

    def find_rows(half):
        def visit(o, group):
            for k, to_req, to_score in group:
                look_up(half, to_req * 16 + to_score, o * 16 + k, k)

        for_peers(visit)
        look_up(half, me, 0, 0)
        got[half, pl.ds(me, 1)] = give[half, 0:1]

    def send_rows(half):
        def visit(o, group):
            for k, to_req, to_score in group:
                pltpu.make_async_remote_copy(
                    src_ref=give.at[half, o * 16 + k],
                    dst_ref=got.at[half, me],
                    send_sem=row_send.at[half],
                    recv_sem=row_recv.at[half],
                    device_id=(to_req, to_score),
                    device_id_type=MESH,
                ).start()

        for_peers(visit)

    def wait_rows(half, sem):
        arrived = got.at[half, pl.ds(0, OWNERS - 1)]
        pltpu.make_async_copy(arrived, arrived, sem.at[half]).wait()

    def find_and_send(half):
        def visit(o, group):
            for k, to_req, to_score in group:
                look_up(half, to_req * 16 + to_score, o * 16 + k, k)
            for k, to_req, to_score in group:
                pltpu.make_async_remote_copy(
                    src_ref=give.at[half, o * 16 + k],
                    dst_ref=got.at[half, me],
                    send_sem=row_send.at[half],
                    recv_sem=row_recv.at[half],
                    device_id=(to_req, to_score),
                    device_id_type=MESH,
                ).start()

        for_peers(visit)
        look_up(half, me, 0, 0)
        got[half, pl.ds(me, 1)] = give[half, 0:1]

    find_and_send(0)
    find_rows(1)

    fifteen = parts.at[pl.ds(0, 15)]
    pltpu.make_async_copy(fifteen, fifteen, user_recv).wait()
    user = jnp.sum(parts[...], axis=0).astype(BF16)
    for copy in large:
        copy.wait()
    user_mixed = jnp.dot(user, cross[0, ITEM:, :], preferred_element_type=F32)
    user32 = user.astype(F32)
    out_w[...] = out_w_ref[...].astype(F32)

    wait_rows(0, row_send)
    send_rows(1)

    def spread(rows, half):
        width = rows.shape[1]
        return jnp.concatenate(
            [jnp.broadcast_to(rows[q:q + 1], (CAND, width)) for q in range(8 * half, 8 * half + 8)],
            axis=0,
        )

    for half in range(2):
        wait_rows(half, row_recv)
        left = got[half, :, 0:SLOTS, :].reshape(OWNERS * SLOTS, 128)
        right = got[half, :, SLOTS:2 * SLOTS, :].reshape(OWNERS * SLOTS, 128)
        found = jnp.concatenate([left, right], axis=1)
        embedded = jnp.dot(
            pick[half * HALF:(half + 1) * HALF, :], found, preferred_element_type=F32
        )
        base = jnp.concatenate([embedded, spread(user32, half)], axis=1)
        mixed = jnp.dot(
            embedded.astype(BF16), cross[0, :ITEM, :], preferred_element_type=F32
        ) + spread(user_mixed, half)
        state = base * mixed + base
        for layer in range(1, CROSS):
            mixed = jnp.dot(state.astype(BF16), cross[layer], preferred_element_type=F32)
            state = base * mixed + state
        state16 = state.astype(BF16)

        def deep_in(n, carry):
            columns = pl.ds(pl.multiple_of(n * 256, 256), 256)
            value = jnp.dot(state16, win[:, columns], preferred_element_type=F32)
            first[:, columns] = jnp.maximum(value, 0.0).astype(BF16)
            return carry

        lax.fori_loop(0, HID // 256, deep_in, 0, unroll=True)

        def deep_mid(n, total):
            columns = pl.ds(pl.multiple_of(n * 256, 256), 256)
            value = jnp.dot(first[...], wmid[:, columns], preferred_element_type=F32)
            second = jnp.maximum(value, 0.0).astype(BF16).astype(F32)
            total += second[:, :128] * out_w[pl.ds(2 * n, 1), :]
            return total + second[:, 128:] * out_w[pl.ds(2 * n + 1, 1), :]

        total = lax.fori_loop(
            0, HID // 256, deep_mid, jnp.zeros((HALF, 128), F32), unroll=True
        )
        scores = jnp.sum(total.T, axis=0, keepdims=True)
        for q in range(8):
            logits_ref[half * 2 + q // 4, pl.ds(q % 4, 1), :] = scores[:, q * CAND:(q + 1) * CAND]

    pltpu.make_async_copy(everything, everything, ask_send).wait()
    pltpu.make_async_copy(fifteen, fifteen, user_send).wait()
    wait_rows(1, row_send)


def on_device(
    owner_ids, local_rows, item_table, user_feats, tower_in, tower_out,
    cross_weights, mlp_in, mlp_mid, mlp_out,
):
    vmem = pl.BlockSpec(memory_space=pltpu.VMEM)
    hbm = pl.BlockSpec(memory_space=pl.ANY)
    dma = pltpu.SemaphoreType.DMA
    return pl.pallas_call(
        kernel,
        out_shape=jax.ShapeDtypeStruct((WINDOWS, REQ_ROWS, CAND), F32),
        in_specs=[vmem] * 4 + [hbm] * 6,
        out_specs=vmem,
        scratch_shapes=[
            pltpu.VMEM((ROWS, ITEM), BF16),
            pltpu.VMEM((2 * ROWS + 8, 128), F32),
            pltpu.VMEM((1024, 128), BF16),
            pltpu.VMEM((128, USER), BF16),
            pltpu.VMEM((CROSS, 512, 512), BF16),
            pltpu.VMEM((512, HID), BF16),
            pltpu.VMEM((HID, HID), BF16),
            pltpu.VMEM((HID // 128, 128), F32),
            pltpu.VMEM((OWNERS, 1, 128), jnp.int32),
            pltpu.VMEM((OWNERS, 1, 128), jnp.int32),
            pltpu.SMEM((OWNERS, 1, 128), jnp.int32),
            pltpu.VMEM((16 * 2 * SLOTS + 8, 128), F32),
            pltpu.VMEM((2, OWNERS, 2 * SLOTS, 128), BF16),
            pltpu.VMEM((2, OWNERS, 2 * SLOTS, 128), BF16),
            pltpu.VMEM((16, USER), F32),
            pltpu.VMEM((16, 16, USER), F32),
            pltpu.VMEM((WINDOWS * BLOCK, OWNERS * SLOTS), BF16),
            pltpu.VMEM((HALF, HID), BF16),
            dma((CHUNKS,)),
            dma((5,)),
            dma((1,)),
            dma,
            dma,
            dma,
            dma,
            dma((2,)),
            dma((2,)),
        ],
        compiler_params=pltpu.CompilerParams(
            collective_id=0, has_side_effects=True, vmem_limit_bytes=60 * 1024 * 1024
        ),
        cost_estimate=pl.CostEstimate(
            flops=13_500_000_000, bytes_accessed=21_000_000, transcendentals=0
        ),
    )(
        owner_ids.reshape(WINDOWS, 1, BLOCK),
        local_rows,
        user_feats,
        mlp_out.reshape(HID // 128, 128),
        item_table,
        tower_in,
        tower_out,
        cross_weights,
        mlp_in,
        mlp_mid,
    )


def solution(mesh):
    in_specs = (
        P("req", "score", None, None, None),
        P(None, "req", "score"),
        P(("req", "score"), None),
        P(None, "req", None),
        P(None, "score"),
        P("score", None),
        P(),
        P(),
        P(),
        P(),
    )
    return jax.shard_map(
        on_device,
        mesh=mesh,
        in_specs=in_specs,
        out_specs=P(None, "req", "score"),
        check_vma=False,
    )
```

```python
import functools

import jax
import jax.numpy as jnp
from jax import lax
from jax.experimental import pallas as pl
from jax.experimental.pallas import tpu as pltpu
from jax.sharding import PartitionSpec as P

CROSS = 3
WINDOWS = 4
BLOCK = 256
REQ_ROWS = 4
CAND = 64
MOST = 3
OWNERS = 128
ROWS = 16384
ITEM = 256
USER = 256
HID = 2048
HALF = 2 * BLOCK
SLOTS = 8
PARTS = ((0, MOST), (MOST, MOST), (2 * MOST, 2 * MOST))
CHUNKS = 8
MESH = pl.DeviceIdType.MESH
F32 = jnp.float32
BF16 = jnp.bfloat16


TURNS = (
    (2, 2), (2, 1), (2, 3), (1, 2), (3, 2), (1, 1), (1, 3), (3, 1),
    (3, 3), (2, 0), (0, 2), (1, 0), (3, 0), (0, 1), (0, 3), (0, 0),
)


def for_peers(visit):
    req, score = lax.axis_index("req"), lax.axis_index("score")
    core = req % 2
    x, y, z = req // 2, score // 4, score % 4
    xs = [((x + d) % 4) * 2 for d in range(4)]
    ys = [((y + d) % 4) * 4 for d in range(4)]
    zs = tuple((z + d) % 4 for d in (2, 2, 1, 1, 3, 3, 0, 0))

    def step(o, carry, last):
        zs, cores = carry
        visit(o, [
            (k, xs[dx] + cores[0], ys[dy] + zs[0]) for k, (dx, dy) in enumerate(TURNS[:last])
        ])
        return zs[1:] + zs[:1], cores[::-1]

    step(7, lax.fori_loop(0, 7, lambda o, carry: step(o, carry, 16), (zs, (1 - core, core))), 15)


def kernel(
    owner_hbm, rows_hbm, feats_hbm, out_w_hbm,
    table_hbm, tin_hbm, tout_hbm, cross_hbm, win_hbm, wmid_hbm,
    logits_ref,
    table, table32, tin, tout, cross, win, wmid,
    owner_ref, rows_ref, feats_ref, out_w_ref,
    out_w, ask, asked, asked_s, stage, give1, got1, give2, got2, part, parts, pick, first,
    load_sem, weight_sem, own_sem, ask_send, ask_recv, user_send, user_recv, row_send, row_recv,
):
    req, score = lax.axis_index("req"), lax.axis_index("score")
    me = req * 16 + score
    chunk = ROWS // CHUNKS

    ids = [
        pltpu.make_async_copy(owner_hbm, owner_ref, own_sem.at[1]),
        pltpu.make_async_copy(rows_hbm, rows_ref, own_sem.at[2]),
    ]
    small = [
        pltpu.make_async_copy(feats_hbm, feats_ref, own_sem.at[3]),
        pltpu.make_async_copy(out_w_hbm, out_w_ref, own_sem.at[4]),
        pltpu.make_async_copy(tin_hbm, tin, weight_sem.at[0]),
        pltpu.make_async_copy(tout_hbm, tout, weight_sem.at[1]),
    ]
    large = [
        pltpu.make_async_copy(cross_hbm, cross, weight_sem.at[2]),
        pltpu.make_async_copy(win_hbm, win, weight_sem.at[3]),
        pltpu.make_async_copy(wmid_hbm, wmid, weight_sem.at[4]),
    ]
    loads = [
        pltpu.make_async_copy(
            table_hbm.at[pl.ds(k * chunk, chunk)], table.at[pl.ds(k * chunk, chunk)], load_sem.at[k]
        )
        for k in range(CHUNKS)
    ]
    for copy in ids + small + loads + large:
        copy.start()

    barrier = pltpu.get_barrier_semaphore()

    def greet(o, group):
        for _, to_req, to_score in group:
            pl.semaphore_signal(barrier, inc=1, device_id=(to_req, to_score), device_id_type=MESH)

    for_peers(greet)

    tri_row = lax.broadcasted_iota(jnp.int32, (BLOCK, BLOCK), 0)
    tri_col = lax.broadcasted_iota(jnp.int32, (BLOCK, BLOCK), 1)
    earlier = jnp.where(tri_row < tri_col, 1.0, 0.0).astype(BF16)
    owner_iota = lax.broadcasted_iota(jnp.int32, (OWNERS, BLOCK), 0)
    high_sum = jnp.zeros((OWNERS, 128), F32)
    low_sum = jnp.zeros((OWNERS, 128), F32)
    places = []
    for copy in ids:
        copy.wait()
    for w in range(WINDOWS):
        owner = owner_ref[w]
        rows = jnp.concatenate([rows_ref[w, r:r + 1, :] for r in range(REQ_ROWS)], axis=1)
        hot = jnp.where(owner_iota == owner, 1.0, 0.0)
        hot16 = hot.astype(BF16)
        before = jnp.dot(hot16, earlier, preferred_element_type=F32)
        slot = jnp.sum(before * hot, axis=0, keepdims=True).astype(jnp.int32)
        at_slot = owner_iota == slot + w * MOST
        high = jnp.where(at_slot, (rows // 128).astype(F32), 0.0).astype(BF16)
        low = jnp.where(at_slot, (rows % 128).astype(F32), 0.0).astype(BF16)
        contract = (((1,), (1,)), ((), ()))
        high_sum += lax.dot_general(hot16, high, contract, preferred_element_type=F32)
        low_sum += lax.dot_general(hot16, low, contract, preferred_element_type=F32)
        if w < 2:
            places += [owner * SLOTS + 2 * slot, owner * SLOTS + 2 * slot + 1]
        else:
            places.append(owner * SLOTS + slot + (w % 2) * MOST)
    asks = (high_sum * 128.0 + low_sum).astype(jnp.int32) * 2
    ask[...] = asks.reshape(OWNERS, 1, 128)

    for copy in small:
        copy.wait()
    feats = jnp.concatenate([feats_ref[w].astype(F32) for w in range(WINDOWS)], axis=0).astype(BF16)
    hidden = jnp.maximum(jnp.dot(feats, tin[...], preferred_element_type=F32), 0.0).astype(BF16)
    part[...] = jnp.dot(hidden, tout[...], preferred_element_type=F32)

    pl.semaphore_wait(barrier, OWNERS - 1)

    def send_ask(o, group):
        for _, to_req, to_score in group:
            pltpu.make_async_remote_copy(
                src_ref=ask.at[to_req * 16 + to_score],
                dst_ref=asked.at[me],
                send_sem=ask_send,
                recv_sem=ask_recv,
                device_id=(to_req, to_score),
                device_id_type=MESH,
            ).start()

    for_peers(send_ask)
    asked[pl.ds(me, 1)] = ask[pl.ds(me, 1)]

    def send_part(step, carry):
        pltpu.make_async_remote_copy(
            src_ref=part,
            dst_ref=parts.at[score],
            send_sem=user_send,
            recv_sem=user_recv,
            device_id=(req, (score + step) % 16),
            device_id_type=MESH,
        ).start()
        return carry

    lax.fori_loop(1, 16, send_part, 0)
    parts[pl.ds(score, 1)] = part[...][None]

    for k in range(CHUNKS):
        loads[k].wait()

        def widen(step, carry):
            base = pl.multiple_of(k * chunk + step * 64, 64)
            block = table[pl.ds(base, 64), :].astype(F32)
            table32[pl.ds(2 * base, 64, stride=2), :] = block[:, :128]
            table32[pl.ds(2 * base + 1, 64, stride=2), :] = block[:, 128:]
            return carry

        lax.fori_loop(0, chunk // 64, widen, 0, unroll=4)

    everything = asked.at[pl.ds(0, OWNERS - 1)]
    pltpu.make_async_copy(everything, everything, ask_recv).wait()
    to_smem = pltpu.make_async_copy(asked, asked_s, own_sem.at[0])
    to_smem.start()

    stage[...] = jnp.zeros_like(stage)
    to_smem.wait()

    def look_up(part_of, to, slot, k):
        base = k * 2 * SLOTS
        first_slot, count = PARTS[part_of]
        for n in range(count):
            at = jnp.clip(asked_s[to, 0, first_slot + n], 0, 2 * ROWS - 2)
            stage[base + 2 * n:base + 2 * n + 2, :] = table32[pl.ds(at, 2), :]
        if part_of < 2:
            give1[part_of, slot] = stage[base:base + SLOTS, :].astype(BF16)
        else:
            give2[slot, 0:SLOTS, :] = stage[pl.ds(base, SLOTS, stride=2), :].astype(BF16)
            give2[slot, SLOTS:2 * SLOTS, :] = stage[pl.ds(base + 1, SLOTS, stride=2), :].astype(BF16)

    gives = [give1.at[0], give1.at[1], give2]
    gots = [got1.at[0], got1.at[1], got2]

    def send_row(part_of, slot, to_req, to_score):
        pltpu.make_async_remote_copy(
            src_ref=gives[part_of].at[slot],
            dst_ref=gots[part_of].at[me],
            send_sem=row_send.at[part_of],
            recv_sem=row_recv.at[part_of],
            device_id=(to_req, to_score),
            device_id_type=MESH,
        ).start()

    def wait_rows(part_of, sem):
        arrived = gots[part_of].at[pl.ds(0, OWNERS - 1)]
        pltpu.make_async_copy(arrived, arrived, sem.at[part_of]).wait()

    def find_and_send(o, group):
        for k, to_req, to_score in group:
            look_up(0, to_req * 16 + to_score, o * 16 + k, k)
        for k, to_req, to_score in group:
            send_row(0, o * 16 + k, to_req, to_score)

    for_peers(find_and_send)

    for part_of in (1, 2):

        def find(o, group):
            for k, to_req, to_score in group:
                look_up(part_of, to_req * 16 + to_score, o * 16 + k, k)

        def send(o, group):
            for k, to_req, to_score in group:
                send_row(part_of, o * 16 + k, to_req, to_score)

        for_peers(find)
        wait_rows(part_of - 1, row_send)
        for_peers(send)

    for part_of in range(3):
        look_up(part_of, me, OWNERS - 1, 15)
    got1[:, pl.ds(me, 1)] = give1[:, OWNERS - 1:OWNERS]
    got2[pl.ds(me, 1)] = give2[OWNERS - 1:OWNERS]

    place = jnp.concatenate(places + [jnp.zeros((2, BLOCK), jnp.int32)], axis=0)
    place_t = place.T
    lane = lax.broadcasted_iota(jnp.int32, (BLOCK, OWNERS * SLOTS), 1)
    for w in range(6):
        pick[w * BLOCK:(w + 1) * BLOCK, :] = jnp.where(
            lane == place_t[:, w:w + 1], 1.0, 0.0
        ).astype(BF16)

    fifteen = parts.at[pl.ds(0, 15)]
    pltpu.make_async_copy(fifteen, fifteen, user_recv).wait()
    user = jnp.sum(parts[...], axis=0).astype(BF16)
    for copy in large:
        copy.wait()
    user_mixed = jnp.dot(user, cross[0, ITEM:, :], preferred_element_type=F32)
    user32 = user.astype(F32)
    out_w[...] = out_w_ref[...].astype(F32)

    def spread(rows, requests):
        width = rows.shape[1]
        return jnp.concatenate(
            [jnp.broadcast_to(rows[q:q + 1], (CAND, width)) for q in requests], axis=0
        )

    def dense(embedded, requests, deep):
        base = jnp.concatenate([embedded, spread(user32, requests)], axis=1)
        mixed = jnp.dot(
            embedded.astype(BF16), cross[0, :ITEM, :], preferred_element_type=F32
        ) + spread(user_mixed, requests)
        state = base * mixed + base
        for layer in range(1, CROSS):
            mixed = jnp.dot(state.astype(BF16), cross[layer], preferred_element_type=F32)
            state = base * mixed + state
        state16 = state.astype(BF16)

        def deep_in(n, carry):
            columns = pl.ds(pl.multiple_of(n * 256, 256), 256)
            value = jnp.dot(state16, win[:, columns], preferred_element_type=F32)
            deep[:, columns] = jnp.maximum(value, 0.0).astype(BF16)
            return carry

        lax.fori_loop(0, HID // 256, deep_in, 0, unroll=True)

        def deep_mid(n, total):
            columns = pl.ds(pl.multiple_of(n * 256, 256), 256)
            value = jnp.dot(deep[...], wmid[:, columns], preferred_element_type=F32)
            second = jnp.maximum(value, 0.0).astype(BF16).astype(F32)
            total += second[:, :128] * out_w[pl.ds(2 * n, 1), :]
            return total + second[:, 128:] * out_w[pl.ds(2 * n + 1, 1), :]

        total = jnp.zeros((len(requests) * CAND, 128), F32)
        total = lax.fori_loop(0, HID // 256, deep_mid, total, unroll=True)
        scores = jnp.sum(total.T, axis=0, keepdims=True)
        for n, q in enumerate(requests):
            logits_ref[q // 4, q % 4:q % 4 + 1, :] = scores[:, n * CAND:(n + 1) * CAND]

    for w in range(2):
        wait_rows(w, row_recv)
        found = got1[w].reshape(OWNERS * SLOTS, 128)
        sides = jnp.dot(
            pick[2 * w * BLOCK:2 * (w + 1) * BLOCK, :], found, preferred_element_type=F32
        )
        embedded = jnp.concatenate([sides[:BLOCK], sides[BLOCK:]], axis=1)
        dense(embedded, range(4 * w, 4 * w + 4), first.at[pl.ds(w * BLOCK, BLOCK)])
    wait_rows(2, row_recv)
    left = got2[:, 0:SLOTS, :].reshape(OWNERS * SLOTS, 128)
    right = got2[:, SLOTS:2 * SLOTS, :].reshape(OWNERS * SLOTS, 128)
    found = jnp.concatenate([left, right], axis=1)
    embedded = jnp.dot(pick[4 * BLOCK:, :], found, preferred_element_type=F32)
    dense(embedded, range(8, 16), first)

    pltpu.make_async_copy(everything, everything, ask_send).wait()
    pltpu.make_async_copy(fifteen, fifteen, user_send).wait()
    wait_rows(2, row_send)


def on_device(
    owner_ids, local_rows, item_table, user_feats, tower_in, tower_out,
    cross_weights, mlp_in, mlp_mid, mlp_out,
):
    vmem = pl.BlockSpec(memory_space=pltpu.VMEM)
    hbm = pl.BlockSpec(memory_space=pl.ANY)
    dma = pltpu.SemaphoreType.DMA
    return pl.pallas_call(
        kernel,
        out_shape=jax.ShapeDtypeStruct((WINDOWS, REQ_ROWS, CAND), F32),
        in_specs=[hbm] * 10,
        out_specs=vmem,
        scratch_shapes=[
            pltpu.VMEM((ROWS, ITEM), BF16),
            pltpu.VMEM((2 * ROWS + 8, 128), F32),
            pltpu.VMEM((1024, 128), BF16),
            pltpu.VMEM((128, USER), BF16),
            pltpu.VMEM((CROSS, 512, 512), BF16),
            pltpu.VMEM((512, HID), BF16),
            pltpu.VMEM((HID, HID), BF16),
            pltpu.VMEM((WINDOWS, 1, BLOCK), jnp.int32),
            pltpu.VMEM((WINDOWS, REQ_ROWS, CAND), jnp.int32),
            pltpu.VMEM((WINDOWS, REQ_ROWS, 1024), BF16),
            pltpu.VMEM((HID // 128, 128), BF16),
            pltpu.VMEM((HID // 128, 128), F32),
            pltpu.VMEM((OWNERS, 1, 128), jnp.int32),
            pltpu.VMEM((OWNERS, 1, 128), jnp.int32),
            pltpu.SMEM((OWNERS, 1, 128), jnp.int32),
            pltpu.VMEM((16 * 2 * SLOTS + 8, 128), F32),
            pltpu.VMEM((2, OWNERS, SLOTS, 128), BF16),
            pltpu.VMEM((2, OWNERS, SLOTS, 128), BF16),
            pltpu.VMEM((OWNERS, 2 * SLOTS, 128), BF16),
            pltpu.VMEM((OWNERS, 2 * SLOTS, 128), BF16),
            pltpu.VMEM((16, USER), F32),
            pltpu.VMEM((16, 16, USER), F32),
            pltpu.VMEM((6 * BLOCK, OWNERS * SLOTS), BF16),
            pltpu.VMEM((HALF, HID), BF16),
            dma((CHUNKS,)),
            dma((5,)),
            dma((5,)),
            dma,
            dma,
            dma,
            dma,
            dma((3,)),
            dma((3,)),
        ],
        compiler_params=pltpu.CompilerParams(
            collective_id=0, has_side_effects=True, vmem_limit_bytes=60 * 1024 * 1024
        ),
        cost_estimate=pl.CostEstimate(
            flops=13_500_000_000, bytes_accessed=21_000_000, transcendentals=0
        ),
    )(
        owner_ids.reshape(WINDOWS, 1, BLOCK),
        local_rows,
        user_feats,
        mlp_out.reshape(HID // 128, 128),
        item_table,
        tower_in,
        tower_out,
        cross_weights,
        mlp_in,
        mlp_mid,
    )


def solution(mesh):
    in_specs = (
        P("req", "score", None, None, None),
        P(None, "req", "score"),
        P(("req", "score"), None),
        P(None, "req", None),
        P(None, "score"),
        P("score", None),
        P(),
        P(),
        P(),
        P(),
    )
    return jax.shard_map(
        on_device,
        mesh=mesh,
        in_specs=in_specs,
        out_specs=P(None, "req", "score"),
        check_vma=False,
    )
```

```python
import functools

import jax
import jax.numpy as jnp
from jax import lax
from jax.experimental import pallas as pl
from jax.experimental.pallas import tpu as pltpu
from jax.sharding import PartitionSpec as P

CROSS = 3
WINDOWS = 4
BLOCK = 256
REQ_ROWS = 4
CAND = 64
MOST = 3
OWNERS = 128
ROWS = 16384
ITEM = 256
USER = 256
HID = 2048
HALF = 2 * BLOCK
SLOTS = 8
PARTS = ((0, MOST), (MOST, MOST), (2 * MOST, 2 * MOST))
CHUNKS = 8
MESH = pl.DeviceIdType.MESH
F32 = jnp.float32
BF16 = jnp.bfloat16


TURNS = (
    (2, 2), (2, 1), (2, 3), (1, 2), (3, 2), (1, 1), (1, 3), (3, 1),
    (3, 3), (2, 0), (0, 2), (1, 0), (3, 0), (0, 1), (0, 3), (0, 0),
)


def for_peers(visit):
    req, score = lax.axis_index("req"), lax.axis_index("score")
    core = req % 2
    x, y, z = req // 2, score // 4, score % 4
    xs = [((x + d) % 4) * 2 for d in range(4)]
    ys = [((y + d) % 4) * 4 for d in range(4)]
    zs = tuple((z + d) % 4 for d in (2, 2, 1, 1, 3, 3, 0, 0))

    def step(o, carry, last):
        zs, cores = carry
        visit(o, [
            (k, xs[dx] + cores[0], ys[dy] + zs[0]) for k, (dx, dy) in enumerate(TURNS[:last])
        ])
        return zs[1:] + zs[:1], cores[::-1]

    step(7, lax.fori_loop(0, 7, lambda o, carry: step(o, carry, 16), (zs, (1 - core, core))), 15)


def kernel(
    owner_hbm, rows_hbm, feats_hbm, out_w_hbm,
    table_hbm, tin_hbm, tout_hbm, cross_hbm, win_hbm, wmid_hbm,
    logits_ref,
    table, table32, tin, tout, cross, win, wmid,
    owner_ref, rows_ref, feats_ref, out_w_ref,
    out_w, ask, asked, asked_s, stage, give1, got1, give2, got2, part, parts, pick, first,
    load_sem, weight_sem, own_sem, ask_send, ask_recv, user_send, user_recv, row_send, row_recv,
):
    req, score = lax.axis_index("req"), lax.axis_index("score")
    me = req * 16 + score
    chunk = ROWS // CHUNKS

    ids = [
        pltpu.make_async_copy(owner_hbm, owner_ref, own_sem.at[1]),
        pltpu.make_async_copy(rows_hbm, rows_ref, own_sem.at[2]),
    ]
    small = [
        pltpu.make_async_copy(feats_hbm, feats_ref, own_sem.at[3]),
        pltpu.make_async_copy(out_w_hbm, out_w_ref, own_sem.at[4]),
        pltpu.make_async_copy(tin_hbm, tin, weight_sem.at[0]),
        pltpu.make_async_copy(tout_hbm, tout, weight_sem.at[1]),
    ]
    large = [
        pltpu.make_async_copy(cross_hbm, cross, weight_sem.at[2]),
        pltpu.make_async_copy(win_hbm, win, weight_sem.at[3]),
        pltpu.make_async_copy(wmid_hbm, wmid, weight_sem.at[4]),
    ]
    loads = [
        pltpu.make_async_copy(
            table_hbm.at[pl.ds(k * chunk, chunk)], table.at[pl.ds(k * chunk, chunk)], load_sem.at[k]
        )
        for k in range(CHUNKS)
    ]
    for copy in ids + small + loads + large:
        copy.start()

    barrier = pltpu.get_barrier_semaphore()

    def greet(o, group):
        for _, to_req, to_score in group:
            pl.semaphore_signal(barrier, inc=1, device_id=(to_req, to_score), device_id_type=MESH)

    for_peers(greet)

    tri_row = lax.broadcasted_iota(jnp.int32, (BLOCK, BLOCK), 0)
    tri_col = lax.broadcasted_iota(jnp.int32, (BLOCK, BLOCK), 1)
    earlier = jnp.where(tri_row < tri_col, 1.0, 0.0).astype(BF16)
    owner_iota = lax.broadcasted_iota(jnp.int32, (OWNERS, BLOCK), 0)
    high_sum = jnp.zeros((OWNERS, 128), F32)
    low_sum = jnp.zeros((OWNERS, 128), F32)
    places = []
    for copy in ids:
        copy.wait()
    for w in range(WINDOWS):
        owner = owner_ref[w]
        rows = jnp.concatenate([rows_ref[w, r:r + 1, :] for r in range(REQ_ROWS)], axis=1)
        hot = jnp.where(owner_iota == owner, 1.0, 0.0)
        hot16 = hot.astype(BF16)
        before = jnp.dot(hot16, earlier, preferred_element_type=F32)
        slot = jnp.sum(before * hot, axis=0, keepdims=True).astype(jnp.int32)
        at_slot = owner_iota == slot + w * MOST
        high = jnp.where(at_slot, (rows // 128).astype(F32), 0.0).astype(BF16)
        low = jnp.where(at_slot, (rows % 128).astype(F32), 0.0).astype(BF16)
        contract = (((1,), (1,)), ((), ()))
        high_sum += lax.dot_general(hot16, high, contract, preferred_element_type=F32)
        low_sum += lax.dot_general(hot16, low, contract, preferred_element_type=F32)
        if w < 2:
            places += [owner * SLOTS + 2 * slot, owner * SLOTS + 2 * slot + 1]
        else:
            places.append(owner * SLOTS + slot + (w % 2) * MOST)
    asks = (high_sum * 128.0 + low_sum).astype(jnp.int32) * 2
    ask[...] = asks.reshape(OWNERS, 1, 128)

    for copy in small:
        copy.wait()
    feats = jnp.concatenate([feats_ref[w].astype(F32) for w in range(WINDOWS)], axis=0).astype(BF16)
    hidden = jnp.maximum(jnp.dot(feats, tin[...], preferred_element_type=F32), 0.0).astype(BF16)
    part[...] = jnp.dot(hidden, tout[...], preferred_element_type=F32)

    pl.semaphore_wait(barrier, OWNERS - 1)

    def send_ask(o, group):
        for _, to_req, to_score in group:
            pltpu.make_async_remote_copy(
                src_ref=ask.at[to_req * 16 + to_score],
                dst_ref=asked.at[me],
                send_sem=ask_send,
                recv_sem=ask_recv,
                device_id=(to_req, to_score),
                device_id_type=MESH,
            ).start()

    for_peers(send_ask)
    asked[pl.ds(me, 1)] = ask[pl.ds(me, 1)]

    def send_part(step, carry):
        pltpu.make_async_remote_copy(
            src_ref=part,
            dst_ref=parts.at[score],
            send_sem=user_send,
            recv_sem=user_recv,
            device_id=(req, (score + step) % 16),
            device_id_type=MESH,
        ).start()
        return carry

    lax.fori_loop(1, 16, send_part, 0)
    parts[pl.ds(score, 1)] = part[...][None]

    for k in range(CHUNKS):
        loads[k].wait()

        def widen(step, carry):
            base = pl.multiple_of(k * chunk + step * 64, 64)
            block = table[pl.ds(base, 64), :].astype(F32)
            table32[pl.ds(2 * base, 64, stride=2), :] = block[:, :128]
            table32[pl.ds(2 * base + 1, 64, stride=2), :] = block[:, 128:]
            return carry

        lax.fori_loop(0, chunk // 64, widen, 0, unroll=4)

    everything = asked.at[pl.ds(0, OWNERS - 1)]
    pltpu.make_async_copy(everything, everything, ask_recv).wait()
    to_smem = pltpu.make_async_copy(asked, asked_s, own_sem.at[0])
    to_smem.start()

    stage[...] = jnp.zeros_like(stage)
    to_smem.wait()

    def look_up(part_of, to, slot, k):
        base = k * 2 * SLOTS
        first_slot, count = PARTS[part_of]
        for n in range(count):
            at = jnp.clip(asked_s[to, 0, first_slot + n], 0, 2 * ROWS - 2)
            stage[base + 2 * n:base + 2 * n + 2, :] = table32[pl.ds(at, 2), :]
        if part_of < 2:
            give1[part_of, slot] = stage[base:base + SLOTS, :].astype(BF16)
        else:
            give2[slot, 0:SLOTS, :] = stage[pl.ds(base, SLOTS, stride=2), :].astype(BF16)
            give2[slot, SLOTS:2 * SLOTS, :] = stage[pl.ds(base + 1, SLOTS, stride=2), :].astype(BF16)

    gives = [give1.at[0], give1.at[1], give2]
    gots = [got1.at[0], got1.at[1], got2]

    def send_row(part_of, slot, to_req, to_score):
        pltpu.make_async_remote_copy(
            src_ref=gives[part_of].at[slot],
            dst_ref=gots[part_of].at[me],
            send_sem=row_send.at[part_of],
            recv_sem=row_recv.at[part_of],
            device_id=(to_req, to_score),
            device_id_type=MESH,
        ).start()

    def wait_rows(part_of, sem):
        arrived = gots[part_of].at[pl.ds(0, OWNERS - 1)]
        pltpu.make_async_copy(arrived, arrived, sem.at[part_of]).wait()

    def find_and_send(o, group):
        for k, to_req, to_score in group:
            look_up(0, to_req * 16 + to_score, o * 16 + k, k)
        for k, to_req, to_score in group:
            send_row(0, o * 16 + k, to_req, to_score)

    for_peers(find_and_send)

    def find_rows(part_of):
        def visit(o, group):
            for k, to_req, to_score in group:
                look_up(part_of, to_req * 16 + to_score, o * 16 + k, k)

        for_peers(visit)

    def send_rows(part_of):
        def visit(o, group):
            for k, to_req, to_score in group:
                send_row(part_of, o * 16 + k, to_req, to_score)

        for_peers(visit)

    find_rows(1)
    place = jnp.concatenate(places + [jnp.zeros((2, BLOCK), jnp.int32)], axis=0)
    place_t = place.T
    lane = lax.broadcasted_iota(jnp.int32, (BLOCK, OWNERS * SLOTS), 1)
    for w in range(6):
        pick[w * BLOCK:(w + 1) * BLOCK, :] = jnp.where(
            lane == place_t[:, w:w + 1], 1.0, 0.0
        ).astype(BF16)

    wait_rows(0, row_send)
    send_rows(1)
    find_rows(2)
    for part_of in range(3):
        look_up(part_of, me, OWNERS - 1, 15)
    got1[:, pl.ds(me, 1)] = give1[:, OWNERS - 1:OWNERS]
    got2[pl.ds(me, 1)] = give2[OWNERS - 1:OWNERS]
    fifteen = parts.at[pl.ds(0, 15)]
    pltpu.make_async_copy(fifteen, fifteen, user_recv).wait()
    user = jnp.sum(parts[...], axis=0).astype(BF16)
    for copy in large:
        copy.wait()
    user_mixed = jnp.dot(user, cross[0, ITEM:, :], preferred_element_type=F32)
    user32 = user.astype(F32)
    out_w[...] = out_w_ref[...].astype(F32)

    wait_rows(1, row_send)
    send_rows(2)

    def spread(rows, requests):
        width = rows.shape[1]
        return jnp.concatenate(
            [jnp.broadcast_to(rows[q:q + 1], (CAND, width)) for q in requests], axis=0
        )

    def dense(embedded, requests, deep):
        base = jnp.concatenate([embedded, spread(user32, requests)], axis=1)
        mixed = jnp.dot(
            embedded.astype(BF16), cross[0, :ITEM, :], preferred_element_type=F32
        ) + spread(user_mixed, requests)
        state = base * mixed + base
        for layer in range(1, CROSS):
            mixed = jnp.dot(state.astype(BF16), cross[layer], preferred_element_type=F32)
            state = base * mixed + state
        state16 = state.astype(BF16)

        def deep_in(n, carry):
            columns = pl.ds(pl.multiple_of(n * 256, 256), 256)
            value = jnp.dot(state16, win[:, columns], preferred_element_type=F32)
            deep[:, columns] = jnp.maximum(value, 0.0).astype(BF16)
            return carry

        lax.fori_loop(0, HID // 256, deep_in, 0, unroll=True)

        def deep_mid(n, total):
            columns = pl.ds(pl.multiple_of(n * 256, 256), 256)
            value = jnp.dot(deep[...], wmid[:, columns], preferred_element_type=F32)
            second = jnp.maximum(value, 0.0).astype(BF16).astype(F32)
            total += second[:, :128] * out_w[pl.ds(2 * n, 1), :]
            return total + second[:, 128:] * out_w[pl.ds(2 * n + 1, 1), :]

        total = jnp.zeros((len(requests) * CAND, 128), F32)
        total = lax.fori_loop(0, HID // 256, deep_mid, total, unroll=True)
        scores = jnp.sum(total.T, axis=0, keepdims=True)
        for n, q in enumerate(requests):
            logits_ref[q // 4, q % 4:q % 4 + 1, :] = scores[:, n * CAND:(n + 1) * CAND]

    for w in range(2):
        wait_rows(w, row_recv)
        found = got1[w].reshape(OWNERS * SLOTS, 128)
        sides = jnp.dot(
            pick[2 * w * BLOCK:2 * (w + 1) * BLOCK, :], found, preferred_element_type=F32
        )
        embedded = jnp.concatenate([sides[:BLOCK], sides[BLOCK:]], axis=1)
        dense(embedded, range(4 * w, 4 * w + 4), first.at[pl.ds(w * BLOCK, BLOCK)])
    wait_rows(2, row_recv)
    left = got2[:, 0:SLOTS, :].reshape(OWNERS * SLOTS, 128)
    right = got2[:, SLOTS:2 * SLOTS, :].reshape(OWNERS * SLOTS, 128)
    found = jnp.concatenate([left, right], axis=1)
    embedded = jnp.dot(pick[4 * BLOCK:, :], found, preferred_element_type=F32)
    dense(embedded, range(8, 16), first)

    pltpu.make_async_copy(everything, everything, ask_send).wait()
    pltpu.make_async_copy(fifteen, fifteen, user_send).wait()
    wait_rows(2, row_send)


def on_device(
    owner_ids, local_rows, item_table, user_feats, tower_in, tower_out,
    cross_weights, mlp_in, mlp_mid, mlp_out,
):
    vmem = pl.BlockSpec(memory_space=pltpu.VMEM)
    hbm = pl.BlockSpec(memory_space=pl.ANY)
    dma = pltpu.SemaphoreType.DMA
    return pl.pallas_call(
        kernel,
        out_shape=jax.ShapeDtypeStruct((WINDOWS, REQ_ROWS, CAND), F32),
        in_specs=[hbm] * 10,
        out_specs=vmem,
        scratch_shapes=[
            pltpu.VMEM((ROWS, ITEM), BF16),
            pltpu.VMEM((2 * ROWS + 8, 128), F32),
            pltpu.VMEM((1024, 128), BF16),
            pltpu.VMEM((128, USER), BF16),
            pltpu.VMEM((CROSS, 512, 512), BF16),
            pltpu.VMEM((512, HID), BF16),
            pltpu.VMEM((HID, HID), BF16),
            pltpu.VMEM((WINDOWS, 1, BLOCK), jnp.int32),
            pltpu.VMEM((WINDOWS, REQ_ROWS, CAND), jnp.int32),
            pltpu.VMEM((WINDOWS, REQ_ROWS, 1024), BF16),
            pltpu.VMEM((HID // 128, 128), BF16),
            pltpu.VMEM((HID // 128, 128), F32),
            pltpu.VMEM((OWNERS, 1, 128), jnp.int32),
            pltpu.VMEM((OWNERS, 1, 128), jnp.int32),
            pltpu.SMEM((OWNERS, 1, 128), jnp.int32),
            pltpu.VMEM((16 * 2 * SLOTS + 8, 128), F32),
            pltpu.VMEM((2, OWNERS, SLOTS, 128), BF16),
            pltpu.VMEM((2, OWNERS, SLOTS, 128), BF16),
            pltpu.VMEM((OWNERS, 2 * SLOTS, 128), BF16),
            pltpu.VMEM((OWNERS, 2 * SLOTS, 128), BF16),
            pltpu.VMEM((16, USER), F32),
            pltpu.VMEM((16, 16, USER), F32),
            pltpu.VMEM((6 * BLOCK, OWNERS * SLOTS), BF16),
            pltpu.VMEM((HALF, HID), BF16),
            dma((CHUNKS,)),
            dma((5,)),
            dma((5,)),
            dma,
            dma,
            dma,
            dma,
            dma((3,)),
            dma((3,)),
        ],
        compiler_params=pltpu.CompilerParams(
            collective_id=0, has_side_effects=True, vmem_limit_bytes=60 * 1024 * 1024
        ),
        cost_estimate=pl.CostEstimate(
            flops=13_500_000_000, bytes_accessed=21_000_000, transcendentals=0
        ),
    )(
        owner_ids.reshape(WINDOWS, 1, BLOCK),
        local_rows,
        user_feats,
        mlp_out.reshape(HID // 128, 128),
        item_table,
        tower_in,
        tower_out,
        cross_weights,
        mlp_in,
        mlp_mid,
    )


def solution(mesh):
    in_specs = (
        P("req", "score", None, None, None),
        P(None, "req", "score"),
        P(("req", "score"), None),
        P(None, "req", None),
        P(None, "score"),
        P("score", None),
        P(),
        P(),
        P(),
        P(),
    )
    return jax.shard_map(
        on_device,
        mesh=mesh,
        in_specs=in_specs,
        out_specs=P(None, "req", "score"),
        check_vma=False,
    )
```

```python
import functools

import jax
import jax.numpy as jnp
from jax import lax
from jax.experimental import pallas as pl
from jax.experimental.pallas import tpu as pltpu
from jax.sharding import PartitionSpec as P

CROSS = 3
WINDOWS = 4
BLOCK = 256
REQ_ROWS = 4
CAND = 64
MOST = 3
OWNERS = 128
ROWS = 16384
ITEM = 256
USER = 256
HID = 2048
HALF = 2 * BLOCK
SLOTS = 8
PARTS = ((0, MOST), (MOST, MOST), (2 * MOST, 2 * MOST))
CHUNKS = 8
MESH = pl.DeviceIdType.MESH
F32 = jnp.float32
BF16 = jnp.bfloat16


TURNS = (
    (2, 2), (2, 1), (2, 3), (1, 2), (3, 2), (1, 1), (1, 3), (3, 1),
    (3, 3), (2, 0), (0, 2), (1, 0), (3, 0), (0, 1), (0, 3), (0, 0),
)


def for_peers(visit):
    req, score = lax.axis_index("req"), lax.axis_index("score")
    core = req % 2
    x, y, z = req // 2, score // 4, score % 4
    xs = [((x + d) % 4) * 2 for d in range(4)]
    ys = [((y + d) % 4) * 4 for d in range(4)]
    zs = tuple((z + d) % 4 for d in (2, 2, 1, 1, 3, 3, 0, 0))

    def step(o, carry, last):
        zs, cores = carry
        visit(o, [
            (k, xs[dx] + cores[0], ys[dy] + zs[0]) for k, (dx, dy) in enumerate(TURNS[:last])
        ])
        return zs[1:] + zs[:1], cores[::-1]

    step(7, lax.fori_loop(0, 7, lambda o, carry: step(o, carry, 16), (zs, (1 - core, core))), 15)


def kernel(
    owner_hbm, rows_hbm, feats_hbm, out_w_hbm,
    table_hbm, tin_hbm, tout_hbm, cross_hbm, win_hbm, wmid_hbm,
    logits_ref,
    table, table32, tin, tout, cross, win, wmid,
    owner_ref, rows_ref, feats_ref, out_w_ref,
    out_w, ask, asked, asked_s, stage, give1, got1, give2, got2, part, parts, pick, first,
    load_sem, weight_sem, own_sem, ask_send, ask_recv, user_send, user_recv, row_send, row_recv,
):
    req, score = lax.axis_index("req"), lax.axis_index("score")
    me = req * 16 + score
    chunk = ROWS // CHUNKS

    ids = [
        pltpu.make_async_copy(owner_hbm, owner_ref, own_sem.at[1]),
        pltpu.make_async_copy(rows_hbm, rows_ref, own_sem.at[2]),
    ]
    small = [
        pltpu.make_async_copy(feats_hbm, feats_ref, own_sem.at[3]),
        pltpu.make_async_copy(out_w_hbm, out_w_ref, own_sem.at[4]),
        pltpu.make_async_copy(tin_hbm, tin, weight_sem.at[0]),
        pltpu.make_async_copy(tout_hbm, tout, weight_sem.at[1]),
    ]
    large = [
        pltpu.make_async_copy(cross_hbm, cross, weight_sem.at[2]),
        pltpu.make_async_copy(win_hbm, win, weight_sem.at[3]),
        pltpu.make_async_copy(wmid_hbm, wmid, weight_sem.at[4]),
    ]
    loads = [
        pltpu.make_async_copy(
            table_hbm.at[pl.ds(k * chunk, chunk)], table.at[pl.ds(k * chunk, chunk)], load_sem.at[k]
        )
        for k in range(CHUNKS)
    ]
    for copy in ids:
        copy.start()

    barrier = pltpu.get_barrier_semaphore()

    def greet(o, group):
        for _, to_req, to_score in group:
            pl.semaphore_signal(barrier, inc=1, device_id=(to_req, to_score), device_id_type=MESH)

    for_peers(greet)
    for copy in small + loads + large:
        copy.start()

    tri_row = lax.broadcasted_iota(jnp.int32, (BLOCK, BLOCK), 0)
    tri_col = lax.broadcasted_iota(jnp.int32, (BLOCK, BLOCK), 1)
    earlier = jnp.where(tri_row < tri_col, 1.0, 0.0).astype(BF16)
    owner_iota = lax.broadcasted_iota(jnp.int32, (OWNERS, BLOCK), 0)
    high_sum = jnp.zeros((OWNERS, 128), F32)
    low_sum = jnp.zeros((OWNERS, 128), F32)
    places = []
    for copy in ids:
        copy.wait()
    for w in range(WINDOWS):
        owner = owner_ref[w]
        rows = jnp.concatenate([rows_ref[w, r:r + 1, :] for r in range(REQ_ROWS)], axis=1)
        hot = jnp.where(owner_iota == owner, 1.0, 0.0)
        hot16 = hot.astype(BF16)
        before = jnp.dot(hot16, earlier, preferred_element_type=F32)
        slot = jnp.sum(before * hot, axis=0, keepdims=True).astype(jnp.int32)
        at_slot = owner_iota == slot + w * MOST
        high = jnp.where(at_slot, (rows // 128).astype(F32), 0.0).astype(BF16)
        low = jnp.where(at_slot, (rows % 128).astype(F32), 0.0).astype(BF16)
        contract = (((1,), (1,)), ((), ()))
        high_sum += lax.dot_general(hot16, high, contract, preferred_element_type=F32)
        low_sum += lax.dot_general(hot16, low, contract, preferred_element_type=F32)
        if w < 2:
            places += [owner * SLOTS + 2 * slot, owner * SLOTS + 2 * slot + 1]
        else:
            places.append(owner * SLOTS + slot + (w % 2) * MOST)
    asks = (high_sum * 128.0 + low_sum).astype(jnp.int32) * 2
    ask[...] = asks.reshape(OWNERS, 1, 128)

    pl.semaphore_wait(barrier, OWNERS - 1)

    def send_ask(o, group):
        for _, to_req, to_score in group:
            pltpu.make_async_remote_copy(
                src_ref=ask.at[to_req * 16 + to_score],
                dst_ref=asked.at[me],
                send_sem=ask_send,
                recv_sem=ask_recv,
                device_id=(to_req, to_score),
                device_id_type=MESH,
            ).start()

    for_peers(send_ask)
    asked[pl.ds(me, 1)] = ask[pl.ds(me, 1)]

    for copy in small:
        copy.wait()
    feats = jnp.concatenate([feats_ref[w].astype(F32) for w in range(WINDOWS)], axis=0).astype(BF16)
    hidden = jnp.maximum(jnp.dot(feats, tin[...], preferred_element_type=F32), 0.0).astype(BF16)
    part[...] = jnp.dot(hidden, tout[...], preferred_element_type=F32)

    def send_part(step, carry):
        pltpu.make_async_remote_copy(
            src_ref=part,
            dst_ref=parts.at[score],
            send_sem=user_send,
            recv_sem=user_recv,
            device_id=(req, (score + step) % 16),
            device_id_type=MESH,
        ).start()
        return carry

    lax.fori_loop(1, 16, send_part, 0)
    parts[pl.ds(score, 1)] = part[...][None]

    for k in range(CHUNKS):
        loads[k].wait()

        def widen(step, carry):
            base = pl.multiple_of(k * chunk + step * 64, 64)
            block = table[pl.ds(base, 64), :].astype(F32)
            table32[pl.ds(2 * base, 64, stride=2), :] = block[:, :128]
            table32[pl.ds(2 * base + 1, 64, stride=2), :] = block[:, 128:]
            return carry

        lax.fori_loop(0, chunk // 64, widen, 0, unroll=4)

    everything = asked.at[pl.ds(0, OWNERS - 1)]
    pltpu.make_async_copy(everything, everything, ask_recv).wait()
    to_smem = pltpu.make_async_copy(asked, asked_s, own_sem.at[0])
    to_smem.start()

    stage[...] = jnp.zeros_like(stage)
    to_smem.wait()

    def look_up(part_of, to, slot, k):
        base = k * 2 * SLOTS
        first_slot, count = PARTS[part_of]
        for n in range(count):
            at = jnp.clip(asked_s[to, 0, first_slot + n], 0, 2 * ROWS - 2)
            stage[base + 2 * n:base + 2 * n + 2, :] = table32[pl.ds(at, 2), :]
        if part_of < 2:
            give1[part_of, slot] = stage[base:base + SLOTS, :].astype(BF16)
        else:
            give2[slot, 0:SLOTS, :] = stage[pl.ds(base, SLOTS, stride=2), :].astype(BF16)
            give2[slot, SLOTS:2 * SLOTS, :] = stage[pl.ds(base + 1, SLOTS, stride=2), :].astype(BF16)

    gives = [give1.at[0], give1.at[1], give2]
    gots = [got1.at[0], got1.at[1], got2]

    def send_row(part_of, slot, to_req, to_score):
        pltpu.make_async_remote_copy(
            src_ref=gives[part_of].at[slot],
            dst_ref=gots[part_of].at[me],
            send_sem=row_send.at[part_of],
            recv_sem=row_recv.at[part_of],
            device_id=(to_req, to_score),
            device_id_type=MESH,
        ).start()

    def wait_rows(part_of, sem):
        arrived = gots[part_of].at[pl.ds(0, OWNERS - 1)]
        pltpu.make_async_copy(arrived, arrived, sem.at[part_of]).wait()

    def find_and_send(o, group):
        for k, to_req, to_score in group:
            look_up(0, to_req * 16 + to_score, o * 16 + k, k)
        for k, to_req, to_score in group:
            send_row(0, o * 16 + k, to_req, to_score)

    for_peers(find_and_send)

    def find_rows(part_of):
        def visit(o, group):
            for k, to_req, to_score in group:
                look_up(part_of, to_req * 16 + to_score, o * 16 + k, k)

        for_peers(visit)

    def send_rows(part_of):
        def visit(o, group):
            for k, to_req, to_score in group:
                send_row(part_of, o * 16 + k, to_req, to_score)

        for_peers(visit)

    find_rows(1)
    place = jnp.concatenate(places + [jnp.zeros((2, BLOCK), jnp.int32)], axis=0)
    place_t = place.T
    lane = lax.broadcasted_iota(jnp.int32, (BLOCK, OWNERS * SLOTS), 1)
    for w in range(6):
        pick[w * BLOCK:(w + 1) * BLOCK, :] = jnp.where(
            lane == place_t[:, w:w + 1], 1.0, 0.0
        ).astype(BF16)

    wait_rows(0, row_send)
    send_rows(1)
    find_rows(2)
    for part_of in range(3):
        look_up(part_of, me, OWNERS - 1, 15)
    got1[:, pl.ds(me, 1)] = give1[:, OWNERS - 1:OWNERS]
    got2[pl.ds(me, 1)] = give2[OWNERS - 1:OWNERS]
    fifteen = parts.at[pl.ds(0, 15)]
    pltpu.make_async_copy(fifteen, fifteen, user_recv).wait()
    user = jnp.sum(parts[...], axis=0).astype(BF16)
    for copy in large:
        copy.wait()
    user_mixed = jnp.dot(user, cross[0, ITEM:, :], preferred_element_type=F32)
    user32 = user.astype(F32)
    out_w[...] = out_w_ref[...].astype(F32)

    wait_rows(1, row_send)
    send_rows(2)

    def spread(rows, requests):
        width = rows.shape[1]
        return jnp.concatenate(
            [jnp.broadcast_to(rows[q:q + 1], (CAND, width)) for q in requests], axis=0
        )

    def dense(embedded, requests, deep):
        base = jnp.concatenate([embedded, spread(user32, requests)], axis=1)
        mixed = jnp.dot(
            embedded.astype(BF16), cross[0, :ITEM, :], preferred_element_type=F32
        ) + spread(user_mixed, requests)
        state = base * mixed + base
        for layer in range(1, CROSS):
            mixed = jnp.dot(state.astype(BF16), cross[layer], preferred_element_type=F32)
            state = base * mixed + state
        state16 = state.astype(BF16)

        def deep_in(n, carry):
            columns = pl.ds(pl.multiple_of(n * 256, 256), 256)
            value = jnp.dot(state16, win[:, columns], preferred_element_type=F32)
            deep[:, columns] = jnp.maximum(value, 0.0).astype(BF16)
            return carry

        lax.fori_loop(0, HID // 256, deep_in, 0, unroll=True)

        def deep_mid(n, total):
            columns = pl.ds(pl.multiple_of(n * 256, 256), 256)
            value = jnp.dot(deep[...], wmid[:, columns], preferred_element_type=F32)
            second = jnp.maximum(value, 0.0).astype(BF16).astype(F32)
            total += second[:, :128] * out_w[pl.ds(2 * n, 1), :]
            return total + second[:, 128:] * out_w[pl.ds(2 * n + 1, 1), :]

        total = jnp.zeros((len(requests) * CAND, 128), F32)
        total = lax.fori_loop(0, HID // 256, deep_mid, total, unroll=True)
        scores = jnp.sum(total.T, axis=0, keepdims=True)
        for n, q in enumerate(requests):
            logits_ref[q // 4, q % 4:q % 4 + 1, :] = scores[:, n * CAND:(n + 1) * CAND]

    for w in range(2):
        wait_rows(w, row_recv)
        found = got1[w].reshape(OWNERS * SLOTS, 128)
        sides = jnp.dot(
            pick[2 * w * BLOCK:2 * (w + 1) * BLOCK, :], found, preferred_element_type=F32
        )
        embedded = jnp.concatenate([sides[:BLOCK], sides[BLOCK:]], axis=1)
        dense(embedded, range(4 * w, 4 * w + 4), first.at[pl.ds(w * BLOCK, BLOCK)])
    wait_rows(2, row_recv)
    left = got2[:, 0:SLOTS, :].reshape(OWNERS * SLOTS, 128)
    right = got2[:, SLOTS:2 * SLOTS, :].reshape(OWNERS * SLOTS, 128)
    found = jnp.concatenate([left, right], axis=1)
    embedded = jnp.dot(pick[4 * BLOCK:, :], found, preferred_element_type=F32)
    dense(embedded, range(8, 16), first)

    pltpu.make_async_copy(everything, everything, ask_send).wait()
    pltpu.make_async_copy(fifteen, fifteen, user_send).wait()
    wait_rows(2, row_send)


def on_device(
    owner_ids, local_rows, item_table, user_feats, tower_in, tower_out,
    cross_weights, mlp_in, mlp_mid, mlp_out,
):
    vmem = pl.BlockSpec(memory_space=pltpu.VMEM)
    hbm = pl.BlockSpec(memory_space=pl.ANY)
    dma = pltpu.SemaphoreType.DMA
    return pl.pallas_call(
        kernel,
        out_shape=jax.ShapeDtypeStruct((WINDOWS, REQ_ROWS, CAND), F32),
        in_specs=[hbm] * 10,
        out_specs=vmem,
        scratch_shapes=[
            pltpu.VMEM((ROWS, ITEM), BF16),
            pltpu.VMEM((2 * ROWS + 8, 128), F32),
            pltpu.VMEM((1024, 128), BF16),
            pltpu.VMEM((128, USER), BF16),
            pltpu.VMEM((CROSS, 512, 512), BF16),
            pltpu.VMEM((512, HID), BF16),
            pltpu.VMEM((HID, HID), BF16),
            pltpu.VMEM((WINDOWS, 1, BLOCK), jnp.int32),
            pltpu.VMEM((WINDOWS, REQ_ROWS, CAND), jnp.int32),
            pltpu.VMEM((WINDOWS, REQ_ROWS, 1024), BF16),
            pltpu.VMEM((HID // 128, 128), BF16),
            pltpu.VMEM((HID // 128, 128), F32),
            pltpu.VMEM((OWNERS, 1, 128), jnp.int32),
            pltpu.VMEM((OWNERS, 1, 128), jnp.int32),
            pltpu.SMEM((OWNERS, 1, 128), jnp.int32),
            pltpu.VMEM((16 * 2 * SLOTS + 8, 128), F32),
            pltpu.VMEM((2, OWNERS, SLOTS, 128), BF16),
            pltpu.VMEM((2, OWNERS, SLOTS, 128), BF16),
            pltpu.VMEM((OWNERS, 2 * SLOTS, 128), BF16),
            pltpu.VMEM((OWNERS, 2 * SLOTS, 128), BF16),
            pltpu.VMEM((16, USER), F32),
            pltpu.VMEM((16, 16, USER), F32),
            pltpu.VMEM((6 * BLOCK, OWNERS * SLOTS), BF16),
            pltpu.VMEM((HALF, HID), BF16),
            dma((CHUNKS,)),
            dma((5,)),
            dma((5,)),
            dma,
            dma,
            dma,
            dma,
            dma((3,)),
            dma((3,)),
        ],
        compiler_params=pltpu.CompilerParams(
            collective_id=0, has_side_effects=True, vmem_limit_bytes=60 * 1024 * 1024
        ),
        cost_estimate=pl.CostEstimate(
            flops=13_500_000_000, bytes_accessed=21_000_000, transcendentals=0
        ),
    )(
        owner_ids.reshape(WINDOWS, 1, BLOCK),
        local_rows,
        user_feats,
        mlp_out.reshape(HID // 128, 128),
        item_table,
        tower_in,
        tower_out,
        cross_weights,
        mlp_in,
        mlp_mid,
    )


def solution(mesh):
    in_specs = (
        P("req", "score", None, None, None),
        P(None, "req", "score"),
        P(("req", "score"), None),
        P(None, "req", None),
        P(None, "score"),
        P("score", None),
        P(),
        P(),
        P(),
        P(),
    )
    return jax.shard_map(
        on_device,
        mesh=mesh,
        in_specs=in_specs,
        out_specs=P(None, "req", "score"),
        check_vma=False,
    )
```
